128 devices in a mesh: row: 8 (over x, core), col: 16 (over z, y).
Axes of the slice: x: 4, y: 4, z: 4, core: 2. Of those that a mesh axis runs over, the one named last changes fastest.
Arguments:
- panel_block: float32 [18432, 128], P(('row', 'col')), may hold values from -160 to 160
- trailing: float32 [18432, 18432], P('row', 'col'), may hold values from -4 to 4
Outputs:
- upper_factor: float32 [128, 128], replicated
- updated: float32 [18432, 18432], P('row', 'col')
The draws below stay inside these ranges and needn't reach their ends.
All inputs are finite; a program needn't handle non-finite values.
Results may differ from the reference program's by a relative error of at most 0.00011.
Values sent between devices are 32-bit elements; how exact they have to be, the bound alone decides.
No kernel may reach another device: no remote copies, remote signals or barrier semaphores. Data moves between devices by JAX's collectives and lax.ppermute only.
A program may use at most 128 MiB of HBM per device.

```python
import math
import jax
import jax.numpy as jnp
from jax import lax

M = 18432
B = 128


def draw_trailing(key, part):
    key = jax.random.fold_in(key, 11)
    base_matrix = jnp.clip(jax.random.normal(key, (M, M), jnp.float32), -4.0, 4.0)
    return (base_matrix + base_matrix.T) * 0.5


def draw_panel_block(key, part):
    key = jax.random.fold_in(key, 5)
    noise_key, row_key, col_key = jax.random.split(key, 3)
    position = jnp.arange(M, dtype=jnp.float32) / M
    row_scale = jnp.exp(math.log(10.0) * (0.5 * position + 0.5 * jax.random.uniform(row_key, (M,), jnp.float32)))
    noise = jnp.clip(jax.random.normal(noise_key, (M, B), jnp.float32), -4.0, 4.0)
    col_scale = jnp.exp(math.log(4.0) * jax.random.uniform(col_key, (B,), jnp.float32))
    return noise * row_scale[:, None] * col_scale[None, :]


def setup_inputs(seed: int = 0) -> dict:
    streams_of = jax.random.split(jax.random.key(seed), 3)
    return {
        "panel_block": draw_panel_block(jax.random.fold_in(streams_of[2], 71), 0),
        "trailing": draw_trailing(jax.random.fold_in(streams_of[2], 71), 0),
    }


precise = lax.Precision.HIGHEST

def reference(panel_block, trailing):
    gram_block = jnp.dot(panel_block.T.astype(jnp.float32), panel_block.astype(jnp.float32), precision=precise, preferred_element_type=jnp.float32)
    upper_factor = jnp.linalg.cholesky(gram_block).T
    basis_rows = jax.scipy.linalg.solve_triangular(upper_factor.T, panel_block.T, lower=True).T
    shifted = basis_rows + jnp.eye(M, B, dtype=panel_block.dtype)
    factor = jnp.linalg.inv(shifted[:B].T)
    image_rows = jnp.dot(trailing, shifted, precision=precise)
    inner_block = jnp.dot(shifted.T, image_rows, precision=precise)
    core_block = jnp.dot(jnp.dot(factor.T, inner_block, precision=precise), factor, precision=precise)
    w_rows = jnp.dot(image_rows, factor, precision=precise) - 0.5 * jnp.dot(shifted, core_block, precision=precise)
    left_side = jnp.concatenate([shifted, w_rows], axis=1)
    right_side = jnp.concatenate([w_rows, shifted], axis=1)
    updated = trailing - jnp.dot(left_side, right_side.T, precision=precise)
    return (upper_factor, updated)
```

```python
import jax
import jax.numpy as jnp
from jax import lax
from jax.experimental import pallas as pl
from jax.experimental.pallas import tpu as pltpu
from jax.sharding import PartitionSpec as P

F32 = jnp.float32
BF16 = jnp.bfloat16
AXES = ("row", "col")
PIECE = 144
WIDTH = 128
ROWS = 16 * PIECE
COLS = 8 * PIECE
TALL = 256
STEPS = ROWS // TALL
VMEM = pl.BlockSpec(memory_space=pltpu.VMEM)
SMEM = pl.BlockSpec(memory_space=pltpu.SMEM)


def pairs(where):
    result = []
    for x in range(4):
        for core in range(2):
            for z in range(4):
                for y in range(4):
                    tx, tcore, tz, ty = where(x, core, z, y)
                    source = (2 * x + core) * 16 + 4 * z + y
                    target = (2 * tx + tcore) * 16 + 4 * tz + ty
                    result.append((source, target))
    return result


def send(value, where):
    return lax.ppermute(value, AXES, pairs(where))


def along_x(k):
    return lambda x, core, z, y: ((x + k) % 4, core, z, y)


def along_z(k):
    return lambda x, core, z, y: (x, core, (z + k) % 4, y)


def along_y(k):
    return lambda x, core, z, y: (x, core, z, (y + k) % 4)


def other_core(x, core, z, y):
    return (x, 1 - core, z, y)


def planes(k):
    return lambda x, core, z, y: (z, core, (x + k) % 4, y)


def to_col_owner(x, core, z, y):
    q = (2 * x + core) * 16 + 4 * z + y
    row, col = q % 8, q // 8
    return (row // 2, row % 2, col // 4, col % 4)


def ring(value, direction):
    return [send(value, direction(k)) for k in (1, 3, 2)]


def halves(value):
    high = value.astype(BF16)
    return high, (value - high.astype(F32)).astype(BF16)


def dot16(left, right, dims):
    return lax.dot_general(left, right, (dims, ((), ())), preferred_element_type=F32)


def split_dot(left, right, dims):
    left_high, left_low = halves(left)
    right_high, right_low = halves(right)
    return (
        dot16(left_low, right_high, dims)
        + dot16(left_high, right_low, dims)
        + dot16(left_high, right_high, dims)
    )


def full_dot(left, right, dims=((1,), (0,))):
    return lax.dot_general(
        left, right, (dims, ((), ())), precision=lax.Precision.HIGHEST, preferred_element_type=F32
    )


def lane(value, index):
    return jnp.take_along_axis(value, jnp.full(value.shape, index, jnp.int32), axis=1)


def rows_of_panel(place, first, near, far, opposite, target):
    z, y = place[2], place[3]
    for kz, block in enumerate((first, near, far, opposite)):
        kz = (0, 1, 3, 2)[kz]
        for ky, slot in ((0, 0), (1, 1), (3, 2), (2, 3)):
            index = ((z - kz) % 4) * 4 + (y - ky) % 4
            start = pl.multiple_of(index * PIECE, 16)
            target[pl.ds(start, PIECE), :] = block[slot * PIECE : (slot + 1) * PIECE, :]


def cols_of_panel(place, own, swapped, target):
    x, core = place[0], place[1]
    for half, block in ((core, own), (1 - core, swapped)):
        for kx, slot in ((0, 0), (1, 1), (3, 2), (2, 3)):
            index = ((x - kx) % 4) * 2 + half
            start = pl.multiple_of(index * PIECE, 16)
            target[pl.ds(start, PIECE), :] = block[slot * PIECE : (slot + 1) * PIECE, :]


def image_kernel(place, trailing, p0, p1, p3, p2, sent, kept, panel_rows, total, corner):
    step = pl.program_id(0)

    @pl.when(step == 0)
    def _():
        rows_of_panel(place, p0, p1, p3, p2, panel_rows)
        total[...] = jnp.zeros_like(total)
        first = jnp.where((place[0] == 0) & (place[1] == 0), 1.0, 0.0)
        corner[...] = trailing[:WIDTH, :].T * first
        gram = full_dot(panel_rows[...], panel_rows[...], ((0,), (0,)))
        top = panel_rows[:WIDTH, :] * first
        for out in (sent, kept):
            out[8 * PIECE : 8 * PIECE + WIDTH, :] = gram
            out[8 * PIECE + WIDTH :, :] = top

    block_high, block_low = halves(trailing[...])
    start = pl.multiple_of(step * TALL, TALL)
    turned_high, turned_low = halves(panel_rows[pl.ds(start, TALL), :].T)
    both = jnp.concatenate([turned_high, turned_low], axis=0)
    wide = dot16(both, block_high, ((1,), (0,)))
    total[...] += wide[:WIDTH] + wide[WIDTH:] + dot16(turned_high, block_low, ((1,), (0,)))

    @pl.when(step == STEPS - 1)
    def _():
        image = total[...].T
        for out, half in ((kept, place[1]), (sent, 1 - place[1])):
            for value in range(2):

                @pl.when(half == value)
                def _(out=out, value=value):
                    for x in range(4):
                        index = (2 * x + value) * PIECE
                        out[x * PIECE : (x + 1) * PIECE, :] = image[index : index + PIECE, :]
                        out[(4 + x) * PIECE : (5 + x) * PIECE, :] = corner[index : index + PIECE, :]


def deal_kernel(place, kept, received, m0, m1, m3, m2):
    x = place[0]
    small = kept[8 * PIECE :, :] + received[8 * PIECE :, :]
    for k, out in ((0, m0), (1, m1), (3, m3), (2, m2)):
        index = (x + k) % 4
        for part in range(2):
            start = pl.multiple_of((4 * part + index) * PIECE, 16)
            rows = pl.ds(start, PIECE)
            out[part * PIECE : (part + 1) * PIECE, :] = kept[rows, :] + received[rows, :]
        out[2 * PIECE :, :] = small


def cholesky_rows(work, factor):
    lanes = lax.broadcasted_iota(jnp.int32, (1, WIDTH), 1)
    subs = lax.broadcasted_iota(jnp.int32, (8, 1), 0)

    def body(t, carry):
        first = pl.multiple_of(8 * t, 8)
        whole = work[...]
        block = work[pl.ds(first, 8), :]
        columns = [lane(whole, first + b) for b in range(8)]
        pivots = [lane(block, first + b) for b in range(8)]
        for i in range(8):
            row, pivot = block[i : i + 1], pivots[i][i : i + 1]
            inverse = 1.0 / pivot
            scaled = row * lax.rsqrt(pivot)
            factor[pl.ds(first + i, 1), :] = jnp.where(lanes >= first + i, scaled, 0.0)
            column, here = pivots[i], subs == i
            row = row * inverse
            block = jnp.where(here, row, block - column * row)
            for b in range(i + 1, 8):
                entry = pivots[b][i : i + 1] * inverse
                pivots[b] = jnp.where(here, entry, pivots[b] - column * entry)
        for i in range(8):
            whole = whole - columns[i] * block[i : i + 1]
        work[...] = whole
        return carry

    lax.fori_loop(0, WIDTH // 8, body, 0)


def factor_kernel(place, own, r1, r3, r2, upper, normal, image, work):
    total = (own[...] + r2[...]) + (r1[...] + r3[...])
    gram = total[2 * PIECE : 2 * PIECE + WIDTH, :]
    work[...] = gram
    cholesky_rows(work, upper)
    factor = upper[...]
    normal[...] = gram + full_dot(total[2 * PIECE + WIDTH :, :], factor, ((0,), (0,)))
    image[...] = total[:PIECE, :] + full_dot(total[PIECE : 2 * PIECE, :], factor)


def inverse_kernel(source, out):
    out[...] = source[...]
    lanes = lax.broadcasted_iota(jnp.int32, (1, WIDTH), 1)
    subs = lax.broadcasted_iota(jnp.int32, (8, 1), 0)

    def body(t, carry):
        first = pl.multiple_of(8 * t, 8)
        whole = out[...]
        block = out[pl.ds(first, 8), :]
        columns = [lane(whole, first + b) for b in range(8)]
        pivots = [lane(block, first + b) for b in range(8)]
        for i in range(8):
            row, column, here = block[i : i + 1], pivots[i], subs == i
            inverse = 1.0 / column[i : i + 1]
            is_lane = lanes == first + i
            row = jnp.where(is_lane, inverse, row * inverse)
            block = jnp.where(here, row, jnp.where(is_lane, 0.0, block) - column * row)
            for b in range(8):
                if b != i:
                    entry = pivots[b][i : i + 1] * inverse
                    pivots[b] = jnp.where(here, entry, pivots[b] - column * entry)
            pivots[i] = jnp.where(here, inverse, -column * inverse)
        whole = jnp.where((lanes >= first) & (lanes < first + 8), 0.0, whole)
        for i in range(8):
            whole = whole - columns[i] * block[i : i + 1]
        out[...] = whole
        out[pl.ds(first, 8), :] = block
        return carry

    lax.fori_loop(0, WIDTH // 8, body, 0)


def pick_kernel(place, b0, b1, b3, b2, out):
    core, y = place[1], place[3]
    for part in range(2):
        wanted = (y - (2 * (1 - core) + part)) % 4
        for k, block in ((0, b0), (1, b1), (3, b3), (2, b2)):

            @pl.when(wanted == k)
            def _(block=block, part=part):
                out[part * 4 * PIECE : (part + 1) * 4 * PIECE, :] = block[...]


def gather_kernel(place, p0, p1, p3, p2, upper, b0, b1, b3, b2, swapped, panel_rows, image_rows, inner):
    x, core, z, y = place[0], place[1], place[2], place[3]
    rows_of_panel(place, p0, p1, p3, p2, panel_rows)
    first = jnp.where((x == 0) & (core == 0), 1.0, 0.0)
    panel_rows[:WIDTH, :] += upper[...] * first

    def put(block, offset, part, half):
        for kz, slot in ((0, 0), (1, 1), (3, 2), (2, 3)):
            index = 8 * part + 2 * ((z - kz) % 4) + half
            start = pl.multiple_of(index * PIECE, 16)
            piece = offset + slot * PIECE
            image_rows[pl.ds(start, PIECE), :] = block[piece : piece + PIECE, :]

    for part in range(2):
        wanted = (y - (2 * core + part)) % 4
        for k, block in ((0, b0), (1, b1), (3, b3), (2, b2)):

            @pl.when(wanted == k)
            def _(block=block, part=part):
                put(block, 0, part, core)

        put(swapped, part * 4 * PIECE, part, 1 - core)
    inner[...] = split_dot(panel_rows[...], image_rows[...], ((0,), (0,)))


def update_kernel(
    place, trailing, panel_rows, image_rows, pc_own, pc_swap, ic_own, ic_swap, upper, inverse,
    k0, k1, k3, k2, out, mixer, right_high, right_low, panel_cols, image_cols,
):
    step = pl.program_id(0)

    @pl.when(step == 0)
    def _():
        inner = (k0[...] + k2[...]) + (k1[...] + k3[...])
        core_block = full_dot(full_dot(inverse[...], inner, ((0,), (0,))), inverse[...])
        mixer[:WIDTH, :] = inverse[...]
        mixer[WIDTH:, :] = -0.5 * core_block
        cols_of_panel(place, pc_own, pc_swap, panel_cols)
        cols_of_panel(place, ic_own, ic_swap, image_cols)
        first = jnp.where((place[2] == 0) & (place[3] == 0), 1.0, 0.0)
        panel_cols[:WIDTH, :] += upper[...] * first
        shifted = panel_cols[...]
        both = jnp.concatenate([image_cols[...], shifted], axis=1)
        w_cols = split_dot(both, mixer[...], ((1,), (0,)))
        right_high[...], right_low[...] = halves(jnp.concatenate([w_cols, shifted], axis=1))

    shifted = panel_rows[...]
    both = jnp.concatenate([image_rows[...], shifted], axis=1)
    w_rows = split_dot(both, mixer[...], ((1,), (0,)))
    left_high, left_low = halves(jnp.concatenate([shifted, w_rows], axis=1))
    dims = ((1,), (1,))
    change = dot16(left_low, right_high[...], dims) + dot16(left_high, right_low[...], dims)
    out[...] = trailing[...] - (change + dot16(left_high, right_high[...], dims))


def shape(rows, columns=WIDTH):
    return jax.ShapeDtypeStruct((rows, columns), F32)


def params(mib):
    return pltpu.CompilerParams(vmem_limit_bytes=mib * 1024 * 1024)


def shards(panel, trailing):
    row, col = lax.axis_index("row"), lax.axis_index("col")
    place = jnp.stack([row // 2, row % 2, col // 4, col % 4]).astype(jnp.int32)

    with jax.named_scope("panel_y"):
        in_y = jnp.concatenate([panel] + ring(panel, along_y), axis=0)
    with jax.named_scope("panel_z"):
        in_z = [in_y] + ring(in_y, along_z)
    with jax.named_scope("panel_columns"):
        piece = send(panel, to_col_owner)
        panel_own = jnp.concatenate([piece] + ring(piece, along_x), axis=0)
        panel_swap = send(panel_own, other_core)

    count = 8 * PIECE + 2 * WIDTH
    with jax.named_scope("image"):
        sent, kept = pl.pallas_call(
            image_kernel,
            grid=(STEPS,),
            in_specs=[SMEM, pl.BlockSpec((TALL, COLS), lambda i: (i, 0))] + [VMEM] * 4,
            out_specs=[VMEM] * 2,
            out_shape=[shape(count)] * 2,
            scratch_shapes=[pltpu.VMEM((ROWS, WIDTH), F32), pltpu.VMEM((WIDTH, COLS), F32), pltpu.VMEM((COLS, WIDTH), F32)],
            compiler_params=params(24),
            cost_estimate=pl.CostEstimate(flops=6 * ROWS * COLS * WIDTH, bytes_accessed=4 * ROWS * COLS, transcendentals=0),
        )(place, trailing, *in_z)
    with jax.named_scope("image_core"):
        received = send(sent, other_core)
    with jax.named_scope("deal"):
        m0, m1, m3, m2 = pl.pallas_call(
            deal_kernel,
            in_specs=[SMEM] + [VMEM] * 2,
            out_specs=[VMEM] * 4,
            out_shape=[shape(2 * PIECE + 2 * WIDTH)] * 4,
            compiler_params=params(8),
        )(place, kept, received)
    with jax.named_scope("image_x"):
        r1, r3, r2 = (send(m, along_x(k)) for m, k in ((m1, 1), (m3, 3), (m2, 2)))
    with jax.named_scope("factor"):
        upper, normal, image = pl.pallas_call(
            factor_kernel,
            in_specs=[SMEM] + [VMEM] * 4,
            out_specs=[VMEM] * 3,
            out_shape=[shape(WIDTH), shape(WIDTH), shape(PIECE)],
            scratch_shapes=[pltpu.VMEM((WIDTH, WIDTH), F32)],
            compiler_params=params(8),
        )(place, m0, r1, r3, r2)

    with jax.named_scope("image_planes"):
        in_plane = jnp.concatenate([send(image, planes(k)) for k in (0, 1, 3, 2)], axis=0)
    with jax.named_scope("image_y"):
        blocks = [in_plane] + ring(in_plane, along_y)
    with jax.named_scope("inverse"):
        inverse = pl.pallas_call(
            inverse_kernel,
            in_specs=[VMEM],
            out_specs=VMEM,
            out_shape=shape(WIDTH),
            compiler_params=params(4),
            cost_estimate=pl.CostEstimate(flops=2000000000, bytes_accessed=131072, transcendentals=0),
        )(normal)
    with jax.named_scope("image_columns"):
        image_own = jnp.concatenate([image] + ring(image, along_x), axis=0)
        image_swap = send(image_own, other_core)
    with jax.named_scope("pick"):
        chosen = pl.pallas_call(
            pick_kernel,
            in_specs=[SMEM] + [VMEM] * 4,
            out_specs=VMEM,
            out_shape=shape(8 * PIECE),
            compiler_params=params(8),
        )(place, *blocks)
    with jax.named_scope("image_swap"):
        swapped = send(chosen, other_core)
    with jax.named_scope("gather"):
        panel_rows, image_rows, inner = pl.pallas_call(
            gather_kernel,
            in_specs=[SMEM] + [VMEM] * 10,
            out_specs=[VMEM] * 3,
            out_shape=[shape(ROWS), shape(ROWS), shape(WIDTH)],
            compiler_params=params(16),
        )(place, *in_z, upper, *blocks, swapped)
    with jax.named_scope("inner"):
        inner = inner + send(inner, other_core)
        k1, k3, k2 = ring(inner, along_x)

    tall = pl.BlockSpec((TALL, WIDTH), lambda i: (i, 0))
    block = pl.BlockSpec((TALL, COLS), lambda i: (i, 0))
    with jax.named_scope("update"):
        updated = pl.pallas_call(
            update_kernel,
            grid=(STEPS,),
            in_specs=[SMEM, block, tall, tall] + [VMEM] * 10,
            out_specs=block,
            out_shape=shape(ROWS, COLS),
            scratch_shapes=[
                pltpu.VMEM((2 * WIDTH, WIDTH), F32),
                pltpu.VMEM((COLS, 2 * WIDTH), BF16),
                pltpu.VMEM((COLS, 2 * WIDTH), BF16),
                pltpu.VMEM((COLS, WIDTH), F32),
                pltpu.VMEM((COLS, WIDTH), F32),
            ],
            compiler_params=params(32),
            cost_estimate=pl.CostEstimate(flops=12 * ROWS * COLS * WIDTH, bytes_accessed=8 * ROWS * COLS, transcendentals=0),
        )(
            place, trailing, panel_rows, image_rows, panel_own, panel_swap, image_own, image_swap, upper, inverse,
            inner, k1, k3, k2,
        )
    return upper, updated


def solution(mesh):
    return jax.shard_map(
        shards,
        mesh=mesh,
        in_specs=(P(("row", "col"), None), P("row", "col")),
        out_specs=(P(), P("row", "col")),
        check_vma=False,
    )
```

```python
import jax
import jax.numpy as jnp
from jax import lax
from jax.experimental import pallas as pl
from jax.experimental.pallas import tpu as pltpu
from jax.sharding import PartitionSpec as P

F32 = jnp.float32
BF16 = jnp.bfloat16
AXES = ("row", "col")
PIECE = 144
WIDTH = 128
ROWS = 16 * PIECE
COLS = 8 * PIECE
TALL = 256
STEPS = ROWS // TALL
VMEM = pl.BlockSpec(memory_space=pltpu.VMEM)
SMEM = pl.BlockSpec(memory_space=pltpu.SMEM)


def pairs(where):
    result = []
    for x in range(4):
        for core in range(2):
            for z in range(4):
                for y in range(4):
                    tx, tcore, tz, ty = where(x, core, z, y)
                    source = (2 * x + core) * 16 + 4 * z + y
                    target = (2 * tx + tcore) * 16 + 4 * tz + ty
                    result.append((source, target))
    return result


def send(value, where):
    return lax.ppermute(value, AXES, pairs(where))


def along_x(k):
    return lambda x, core, z, y: ((x + k) % 4, core, z, y)


def along_z(k):
    return lambda x, core, z, y: (x, core, (z + k) % 4, y)


def along_y(k):
    return lambda x, core, z, y: (x, core, z, (y + k) % 4)


def other_core(x, core, z, y):
    return (x, 1 - core, z, y)


def planes(k):
    return lambda x, core, z, y: (z, core, (x + k) % 4, y)


def ring(value, direction):
    return [send(value, direction(k)) for k in (1, 3, 2)]


def halves(value):
    high = value.astype(BF16)
    return high, (value - high.astype(F32)).astype(BF16)


def dot16(left, right, dims):
    return lax.dot_general(left, right, (dims, ((), ())), preferred_element_type=F32)


def split_dot(left, right, dims):
    left_high, left_low = halves(left)
    right_high, right_low = halves(right)
    return (
        dot16(left_low, right_high, dims)
        + dot16(left_high, right_low, dims)
        + dot16(left_high, right_high, dims)
    )


def full_dot(left, right, dims=((1,), (0,))):
    return lax.dot_general(
        left, right, (dims, ((), ())), precision=lax.Precision.HIGHEST, preferred_element_type=F32
    )


def lane(value, index):
    return jnp.take_along_axis(value, jnp.full(value.shape, index, jnp.int32), axis=1)


ALONG = (0, 1, 3, 2)


def around(core):
    return (0, 1 + 2 * core, 3 - 2 * core, 2)


def put_in_order(at, steps, pieces, out, rows, first=0):
    for k, piece in zip(steps, pieces):
        start = pl.multiple_of(first + ((at - k + 4) % 4) * rows, 16)
        out[pl.ds(start, rows), :] = piece[...]


def join_y_kernel(place, p0, p1, p3, p2, out):
    put_in_order(place[3], ALONG, (p0, p1, p3, p2), out, PIECE)


def join_z_kernel(place, p0, p1, p3, p2, out):
    put_in_order(place[2], ALONG, (p0, p1, p3, p2), out, PIECE)


def hand_kernel(place, across, out):
    out[...] = across[pl.ds(pl.multiple_of((1 - place[1]) * PIECE, 16), PIECE), :]


def tag_kernel(place, image, across, handed, out):
    out[:PIECE, :] = image[...]

    @pl.when(place[3] // 2 == place[1])
    def _():
        out[PIECE:, :] = across[pl.ds(pl.multiple_of(place[1] * PIECE, 16), PIECE), :]

    @pl.when(place[3] // 2 != place[1])
    def _():
        out[PIECE:, :] = handed[...]


def split_kernel(trailing, after, whole, high, low, sems):
    copies = []
    for i in range(STEPS):
        rows = pl.ds(i * TALL, TALL)
        copies.append(pltpu.make_async_copy(trailing.at[rows, :], whole.at[rows, :], sems.at[i]))
        copies[-1].start()
    for i in range(STEPS):
        copies[i].wait()
        rows = slice(i * TALL, (i + 1) * TALL)
        high[rows, :], low[rows, :] = halves(whole[rows, :])


def turned_image(place, k, block, high, low):
    rows = pl.ds(pl.multiple_of(((place[2] - k + 4) % 4) * 4 * PIECE, 16), 4 * PIECE)
    turned_high, turned_low = halves(block[...].T)
    wide = dot16(jnp.concatenate([turned_high, turned_low], axis=0), high[rows, :], ((1,), (0,)))
    return wide[:WIDTH] + wide[WIDTH:] + dot16(turned_high, low[rows, :], ((1,), (0,)))


def near_kernel(place, high, low, own, front, back, image, gram, gram_near):
    total = jnp.zeros((WIDTH, COLS), F32)
    for k, block in zip(around(place[1]), (own, front, back)):
        total += turned_image(place, k, block, high, low)
    image[...] = total
    gram[...] = full_dot(own[...], own[...], ((0,), (0,)))
    gram_near[...] = full_dot(front[...], front[...], ((0,), (0,))) + full_dot(back[...], back[...], ((0,), (0,)))


def far_gram_kernel(place, own, below, above, far, gram, gram_near, out):
    x, core, z = place[0], place[1], place[2]
    out[:WIDTH, :] = (gram[...] + full_dot(far[...], far[...], ((0,), (0,)))) + gram_near[...]
    out[WIDTH:, :] = jnp.zeros((WIDTH, WIDTH), F32)
    for k, block in zip(around(core), (own, below, above, far)):

        @pl.when((x == 0) & (core == 0) & (z == k))
        def _(block=block):
            out[WIDTH:, :] = block[:WIDTH, :]


def image_kernel(place, whole, high, low, near, own, front, back, far, sent, kept, across):
    image = (near[...] + turned_image(place, 2, far, high, low)).T
    block, half = 2 * (place[3] % 2) + place[2] // 2, place[2] % 2
    for k, piece in zip(around(place[1]), (own, front, back, far)):

        @pl.when((place[2] - k + 4) % 4 == block)
        def _(piece=piece):
            across[...] = piece[pl.ds(pl.multiple_of(half * 2 * PIECE, 16), 2 * PIECE), :]

    corner = whole[:WIDTH, :].T * jnp.where((place[0] == 0) & (place[1] == 0), 1.0, 0.0)
    for out, half in ((kept, place[1]), (sent, 1 - place[1])):
        for value in range(2):

            @pl.when(half == value)
            def _(out=out, value=value):
                for x in range(4):
                    index = (2 * x + value) * PIECE
                    out[x * PIECE : (x + 1) * PIECE, :] = image[index : index + PIECE, :]
                    out[(4 + x) * PIECE : (5 + x) * PIECE, :] = corner[index : index + PIECE, :]


def factor_kernel(g0, g1, g3, g2, upper, upper_here, normal, work):
    total = (g0[...] + g2[...]) + (g1[...] + g3[...])
    work[...] = total[:WIDTH, :]
    cholesky_rows(work, upper_here)
    factor = upper_here[...]
    upper[...] = factor
    normal[...] = total[:WIDTH, :] + full_dot(total[WIDTH:, :], factor, ((0,), (0,)))


def deal_kernel(place, kept, received, upper, m0, m1, m3, m2, image):
    half = kept[...] + received[...]
    image[...] = half[: 4 * PIECE, :] + split_dot(half[4 * PIECE :, :], upper[...], ((1,), (0,)))
    for k, out in ((0, m0), (1, m1), (3, m3), (2, m2)):
        start = pl.multiple_of(((place[0] + k) % 4) * PIECE, 16)
        out[...] = image[pl.ds(start, PIECE), :]


def sum_kernel(own, r1, r3, r2, image):
    image[...] = (own[...] + r2[...]) + (r1[...] + r3[...])


def untag_kernel(place, p0, p1, p3, p2, out):
    pieces = (p0, p1, p3, p2)
    put_in_order(place[0], ALONG, [p.at[:PIECE, :] for p in pieces], out, PIECE)
    put_in_order(place[0], ALONG, [p.at[PIECE:, :] for p in pieces], out, PIECE, 4 * PIECE)


def cholesky_rows(work, factor):
    lanes = lax.broadcasted_iota(jnp.int32, (1, WIDTH), 1)
    subs = lax.broadcasted_iota(jnp.int32, (8, 1), 0)

    def body(t, carry):
        first = pl.multiple_of(8 * t, 8)
        whole = work[...]
        block = work[pl.ds(first, 8), :]
        columns = [lane(whole, first + b) for b in range(8)]
        pivots = [lane(block, first + b) for b in range(8)]
        for i in range(8):
            row, pivot = block[i : i + 1], pivots[i][i : i + 1]
            inverse = 1.0 / pivot
            scaled = row * lax.rsqrt(pivot)
            factor[pl.ds(first + i, 1), :] = jnp.where(lanes >= first + i, scaled, 0.0)
            column, here = pivots[i], subs == i
            row = row * inverse
            block = jnp.where(here, row, block - column * row)
            for b in range(i + 1, 8):
                entry = pivots[b][i : i + 1] * inverse
                pivots[b] = jnp.where(here, entry, pivots[b] - column * entry)
        for i in range(8):
            whole = whole - columns[i] * block[i : i + 1]
        work[...] = whole
        return carry

    lax.fori_loop(0, WIDTH // 8, body, 0)


def inverse_kernel(source, out):
    out[...] = source[...]
    lanes = lax.broadcasted_iota(jnp.int32, (1, WIDTH), 1)
    subs = lax.broadcasted_iota(jnp.int32, (8, 1), 0)

    def body(t, carry):
        first = pl.multiple_of(8 * t, 8)
        whole = out[...]
        block = out[pl.ds(first, 8), :]
        columns = [lane(whole, first + b) for b in range(8)]
        pivots = [lane(block, first + b) for b in range(8)]
        for i in range(8):
            row, column, here = block[i : i + 1], pivots[i], subs == i
            inverse = 1.0 / column[i : i + 1]
            is_lane = lanes == first + i
            row = jnp.where(is_lane, inverse, row * inverse)
            block = jnp.where(here, row, jnp.where(is_lane, 0.0, block) - column * row)
            for b in range(8):
                if b != i:
                    entry = pivots[b][i : i + 1] * inverse
                    pivots[b] = jnp.where(here, entry, pivots[b] - column * entry)
            pivots[i] = jnp.where(here, inverse, -column * inverse)
        whole = jnp.where((lanes >= first) & (lanes < first + 8), 0.0, whole)
        for i in range(8):
            whole = whole - columns[i] * block[i : i + 1]
        out[...] = whole
        out[pl.ds(first, 8), :] = block
        return carry

    lax.fori_loop(0, WIDTH // 8, body, 0)


def pick_kernel(place, b0, b1, b3, b2, out):
    core, y = place[1], place[3]
    for part in range(2):
        wanted = (y - (2 * (1 - core) + part) + 4) % 4
        for k, block in zip(around(core), (b0, b1, b3, b2)):

            @pl.when(wanted == k)
            def _(block=block, part=part):
                out[part * 4 * PIECE : (part + 1) * 4 * PIECE, :] = block[...]


def gather_kernel(place, p0, p1, p3, p2, upper, b0, b1, b3, b2, swapped, shifted, image_rows, inner):
    x, core, z, y = place[0], place[1], place[2], place[3]
    first = jnp.where((x == 0) & (core == 0), 1.0, 0.0)
    put_in_order(z, around(core), (p0, p1, p3, p2), shifted, 4 * PIECE)
    shifted[:WIDTH, :] += upper[...] * first

    def put(block, offset, part, half):
        for other in range(4):
            start = pl.multiple_of((8 * part + 2 * other + half) * PIECE, 16)
            piece = offset + other * PIECE
            image_rows[pl.ds(start, PIECE), :] = block[piece : piece + PIECE, :]

    for part in range(2):
        wanted = (y - (2 * core + part) + 4) % 4
        for k, block in zip(around(core), (b0, b1, b3, b2)):

            @pl.when(wanted == k)
            def _(block=block, part=part):
                put(block, 0, part, core)

        put(swapped, part * 4 * PIECE, part, 1 - core)
    inner[...] = split_dot(shifted[...], image_rows[...], ((0,), (0,)))


def cols_of(place, own, swapped, target, part):
    for half, block in ((place[1], own), (1 - place[1], swapped)):
        for x in range(4):
            start = pl.multiple_of((2 * x + half) * PIECE, 16)
            piece = (4 * part + x) * PIECE
            target[pl.ds(start, PIECE), :] = block[piece : piece + PIECE, :]


def wide_dot(left, right):
    left_high, left_low = halves(left)
    right_high, right_low = halves(right)
    width = right.shape[1]
    both = dot16(left_high, jnp.concatenate([right_high, right_low], axis=1), ((1,), (0,)))
    return both[:, :width] + both[:, width:] + dot16(left_low, right_high, ((1,), (0,)))


def first_update_kernel(
    place, whole, shifted_rows, image_rows, own, swapped, upper, inverse,
    result, turned, panel_cols, image_cols, right_high, right_low, w_rows,
):
    cols_of(place, own, swapped, image_cols, 0)
    cols_of(place, own, swapped, panel_cols, 1)
    first = jnp.where((place[2] == 0) & (place[3] == 0), 1.0, 0.0)
    panel_cols[:WIDTH, :] += upper[...] * first
    turned[...] = panel_cols[...].T
    w_cols = wide_dot(image_cols[...], inverse[...])
    right_high[:WIDTH, :], right_low[:WIDTH, :] = halves(w_cols.T)
    right_high[WIDTH:, :], right_low[WIDTH:, :] = halves(turned[...])
    w_rows[...] = wide_dot(image_rows[...], inverse[...])
    dims = ((1,), (0,))
    for i in range(ROWS // WIDTH):
        rows = slice(i * WIDTH, (i + 1) * WIDTH)
        left_high, left_low = halves(jnp.concatenate([shifted_rows[rows, :], w_rows[rows, :]], axis=1))
        change = dot16(left_low, right_high[...], dims) + dot16(left_high, right_low[...], dims)
        result[rows, :] = whole[rows, :] - (change + dot16(left_high, right_high[...], dims))


def last_update_kernel(base, shifted_rows, turned, inverse, k0, k1, k3, k2, out, right, right_low, result, sems):
    inner = (k0[...] + k2[...]) + (k1[...] + k3[...])
    dims = ((1,), (0,))
    core_block = split_dot(split_dot(inverse[...], inner, ((0,), (0,))), inverse[...], dims)
    high, low = halves(split_dot(core_block, turned[...], dims))
    right[:WIDTH, :] = high
    right[WIDTH:, :] = high
    right_low[...] = low
    copies = []
    for i in range(ROWS // WIDTH):
        rows = slice(i * WIDTH, (i + 1) * WIDTH)
        left_high, left_low = halves(shifted_rows[rows, :])
        change = dot16(jnp.concatenate([left_high, left_low], axis=1), right[...], dims)
        result[rows, :] = base[rows, :] + (change + dot16(left_high, right_low[...], dims))
        rows = pl.ds(i * WIDTH, WIDTH)
        copies.append(pltpu.make_async_copy(result.at[rows, :], out.at[rows, :], sems.at[i]))
        copies[-1].start()
    for copy in copies:
        copy.wait()


def shape(rows, columns=WIDTH):
    return jax.ShapeDtypeStruct((rows, columns), F32)


def params(mib):
    return pltpu.CompilerParams(vmem_limit_bytes=mib * 1024 * 1024)


def local(kernel, out_shape, mib, scratch=(), flops=0):
    cost = pl.CostEstimate(flops=flops, bytes_accessed=0, transcendentals=0) if flops else None

    def run(*operands):
        specs = [SMEM if value.dtype == jnp.int32 else VMEM for value in operands]
        outs = [VMEM] * len(out_shape) if isinstance(out_shape, list) else VMEM
        return pl.pallas_call(
            kernel, in_specs=specs, out_specs=outs, out_shape=out_shape, scratch_shapes=list(scratch),
            compiler_params=params(mib), cost_estimate=cost,
        )(*operands)

    return run


def turn(axis, first):
    def where(x, core, z, y):
        return axis(first if core == 0 else 4 - first)(x, core, z, y)

    return where


def after(values, *earlier):
    return lax.optimization_barrier((values, earlier))[0]


def shards(panel, trailing):
    row, col = lax.axis_index("row"), lax.axis_index("col")
    place = jnp.stack([row // 2, row % 2, col // 4, col % 4]).astype(jnp.int32)
    anywhere = pl.BlockSpec(memory_space=pl.ANY)
    tile = shape(WIDTH)
    tile16 = jax.ShapeDtypeStruct((ROWS, COLS), BF16)

    with jax.named_scope("panel_y"):
        in_y = local(join_y_kernel, shape(4 * PIECE), 4)(place, panel, *ring(panel, along_y))
    with jax.named_scope("panel_z"):
        below, above = send(in_y, turn(along_z, 1)), send(in_y, turn(along_z, 3))
    with jax.named_scope("split"):
        whole, high, low = pl.pallas_call(
            split_kernel,
            in_specs=[anywhere, VMEM],
            out_specs=[VMEM] * 3,
            out_shape=[shape(ROWS, COLS), tile16, tile16],
            scratch_shapes=[pltpu.SemaphoreType.DMA((STEPS,))],
            compiler_params=params(24),
            cost_estimate=pl.CostEstimate(flops=0, bytes_accessed=4 * ROWS * COLS, transcendentals=0),
        )(trailing, in_y)
    below, above = after((below, above), whole)
    with jax.named_scope("panel_far"):
        far = send(below, turn(along_z, 1))
    with jax.named_scope("near"):
        near, gram, gram_near = local(near_kernel, [shape(WIDTH, COLS), tile, tile], 16, flops=5 * ROWS * COLS * WIDTH)(
            place, high, low, in_y, below, above
        )
    far = after(far, gram)
    in_z = [in_y, below, above, far]

    with jax.named_scope("gram"):
        gram = local(far_gram_kernel, shape(2 * WIDTH), 4)(place, *in_z, gram, gram_near)
    with jax.named_scope("gram_sum"):
        gram = gram + send(gram, other_core)
        grams = [gram] + ring(gram, along_x)
    with jax.named_scope("image"):
        sent, kept, across = local(
            image_kernel, [shape(8 * PIECE)] * 2 + [shape(2 * PIECE)], 24, flops=2 * ROWS * COLS * WIDTH
        )(place, whole, high, low, near, *after(in_z, gram))
    grams = after(grams, kept)
    with jax.named_scope("image_core"):
        received = send(after(sent, grams), other_core)
    with jax.named_scope("panel_across"):
        across = send(after(across, grams), planes(0))
    with jax.named_scope("factor"):
        upper, upper_here, normal = local(factor_kernel, [tile] * 3, 4, [pltpu.VMEM((WIDTH, WIDTH), F32)], 2000000000)(
            *grams
        )
    with jax.named_scope("deal"):
        m0, m1, m3, m2 = local(deal_kernel, [shape(PIECE)] * 4, 8, [pltpu.VMEM((4 * PIECE, WIDTH), F32)])(
            place, kept, received, upper_here
        )
    with jax.named_scope("image_x"):
        r1, r3, r2 = (send(m, along_x(k)) for m, k in ((m1, 1), (m3, 3), (m2, 2)))
    with jax.named_scope("panel_across"):
        handed = send(local(hand_kernel, shape(PIECE), 4)(place, after(across, m0)), other_core)
    r1, r3, r2, handed = after((r1, r3, r2, handed))
    with jax.named_scope("image_x"):
        image = local(sum_kernel, shape(PIECE), 4)(m0, r1, r3, r2)

    with jax.named_scope("image_planes"):
        planes_in = [send(image, planes(k)) for k in (0, 1, 3, 2)]
        in_plane = local(join_z_kernel, shape(4 * PIECE), 4)(place, *planes_in)
    with jax.named_scope("image_y"):
        below, above = send(in_plane, turn(along_y, 1)), send(in_plane, turn(along_y, 3))
    with jax.named_scope("image_columns"):
        tagged = local(tag_kernel, shape(2 * PIECE), 4)(place, image, across, after(handed, in_plane))
    with jax.named_scope("inverse"):
        inverse = local(inverse_kernel, tile, 4, flops=2000000000)(after(normal, in_plane))
    below, tagged = after((below, tagged), inverse)
    with jax.named_scope("image_far"):
        opposite = send(below, turn(along_y, 1))
    with jax.named_scope("image_columns"):
        sides = ring(after(tagged, below), along_x)
    blocks = [in_plane, below, above, opposite]
    with jax.named_scope("pick"):
        chosen = local(pick_kernel, shape(8 * PIECE), 8)(place, *blocks)
    with jax.named_scope("image_swap"):
        swapped = send(chosen, other_core)
    with jax.named_scope("image_columns"):
        own = local(untag_kernel, shape(8 * PIECE), 8)(place, tagged, *after(sides, chosen))
        other = send(own, other_core)
    with jax.named_scope("gather"):
        shifted, image_rows, inner = local(gather_kernel, [shape(ROWS), shape(ROWS), tile], 16)(
            place, *in_z, upper_here, *blocks, swapped
        )
    with jax.named_scope("inner"):
        inner = inner + send(inner, other_core)
        k1, k3, k2 = ring(inner, along_x)

    with jax.named_scope("first_update"):
        base, turned = local(
            first_update_kernel,
            [shape(ROWS, COLS), shape(WIDTH, COLS)],
            24,
            [
                pltpu.VMEM((COLS, WIDTH), F32),
                pltpu.VMEM((COLS, WIDTH), F32),
                pltpu.VMEM((2 * WIDTH, COLS), BF16),
                pltpu.VMEM((2 * WIDTH, COLS), BF16),
                pltpu.VMEM((ROWS, WIDTH), F32),
            ],
            12 * ROWS * COLS * WIDTH,
        )(place, whole, shifted, image_rows, own, other, upper_here, after(inverse, inner))
    k1, k3, k2 = after((k1, k3, k2), base)
    with jax.named_scope("last_update"):
        updated = pl.pallas_call(
            last_update_kernel,
            in_specs=[VMEM] * 8,
            out_specs=anywhere,
            out_shape=shape(ROWS, COLS),
            scratch_shapes=[
                pltpu.VMEM((2 * WIDTH, COLS), BF16),
                pltpu.VMEM((WIDTH, COLS), BF16),
                pltpu.VMEM((ROWS, COLS), F32),
                pltpu.SemaphoreType.DMA((ROWS // WIDTH,)),
            ],
            compiler_params=params(20),
            cost_estimate=pl.CostEstimate(flops=8 * ROWS * COLS * WIDTH, bytes_accessed=4 * ROWS * COLS, transcendentals=0),
        )(base, shifted, turned, inverse, inner, k1, k3, k2)
    return upper, updated


def solution(mesh):
    return jax.shard_map(
        shards,
        mesh=mesh,
        in_specs=(P(("row", "col"), None), P("row", "col")),
        out_specs=(P(), P("row", "col")),
        check_vma=False,
    )
```

```python
import jax
import jax.numpy as jnp
from jax import lax
from jax.experimental import pallas as pl
from jax.experimental.pallas import tpu as pltpu
from jax.sharding import PartitionSpec as P

F32 = jnp.float32
BF16 = jnp.bfloat16
AXES = ("row", "col")
PIECE = 144
WIDTH = 128
ROWS = 16 * PIECE
COLS = 8 * PIECE
TALL = 256
STEPS = ROWS // TALL
VMEM = pl.BlockSpec(memory_space=pltpu.VMEM)
SMEM = pl.BlockSpec(memory_space=pltpu.SMEM)


def pairs(where):
    result = []
    for x in range(4):
        for core in range(2):
            for z in range(4):
                for y in range(4):
                    tx, tcore, tz, ty = where(x, core, z, y)
                    source = (2 * x + core) * 16 + 4 * z + y
                    target = (2 * tx + tcore) * 16 + 4 * tz + ty
                    result.append((source, target))
    return result


def send(value, where):
    return lax.ppermute(value, AXES, pairs(where))


def along_x(k):
    return lambda x, core, z, y: ((x + k) % 4, core, z, y)


def along_z(k):
    return lambda x, core, z, y: (x, core, (z + k) % 4, y)


def along_y(k):
    return lambda x, core, z, y: (x, core, z, (y + k) % 4)


def other_core(x, core, z, y):
    return (x, 1 - core, z, y)


def planes(k):
    return lambda x, core, z, y: (z, core, (x + k) % 4, y)


def ring(value, direction):
    return [send(value, direction(k)) for k in (1, 3, 2)]


def halves(value):
    high = value.astype(BF16)
    return high, (value - high.astype(F32)).astype(BF16)


def dot16(left, right, dims):
    return lax.dot_general(left, right, (dims, ((), ())), preferred_element_type=F32)


def split_dot(left, right, dims):
    left_high, left_low = halves(left)
    right_high, right_low = halves(right)
    return (
        dot16(left_low, right_high, dims)
        + dot16(left_high, right_low, dims)
        + dot16(left_high, right_high, dims)
    )


def full_dot(left, right, dims=((1,), (0,))):
    return lax.dot_general(
        left, right, (dims, ((), ())), precision=lax.Precision.HIGHEST, preferred_element_type=F32
    )


def lane(value, index):
    return jnp.take_along_axis(value, jnp.full(value.shape, index, jnp.int32), axis=1)


ALONG = (0, 1, 3, 2)


def around(core):
    return (0, 1 + 2 * core, 3 - 2 * core, 2)


def put_in_order(at, steps, pieces, out, rows, first=0):
    for k, piece in zip(steps, pieces):
        start = pl.multiple_of(first + ((at - k + 4) % 4) * rows, 16)
        out[pl.ds(start, rows), :] = piece[...]


def join_y_kernel(place, p0, p1, p3, p2, out):
    put_in_order(place[3], ALONG, (p0, p1, p3, p2), out, PIECE)


def join_z_kernel(place, p0, p1, p3, p2, out):
    put_in_order(place[2], ALONG, (p0, p1, p3, p2), out, PIECE)


def hand_kernel(place, across, out):
    out[...] = across[pl.ds(pl.multiple_of((1 - place[1]) * PIECE, 16), PIECE), :]


def tag_kernel(place, image, across, handed, out):
    out[:PIECE, :] = image[...]

    @pl.when(place[3] // 2 == place[1])
    def _():
        out[PIECE:, :] = across[pl.ds(pl.multiple_of(place[1] * PIECE, 16), PIECE), :]

    @pl.when(place[3] // 2 != place[1])
    def _():
        out[PIECE:, :] = handed[...]


def split_kernel(trailing, after, whole, high, low, sems):
    copies = []
    for i in range(STEPS):
        rows = pl.ds(i * TALL, TALL)
        copies.append(pltpu.make_async_copy(trailing.at[rows, :], whole.at[rows, :], sems.at[i]))
        copies[-1].start()
    for i in range(STEPS):
        copies[i].wait()
        rows = slice(i * TALL, (i + 1) * TALL)
        high[rows, :], low[rows, :] = halves(whole[rows, :])


def turned_image(place, k, block, high, low):
    rows = pl.ds(pl.multiple_of(((place[2] - k + 4) % 4) * 4 * PIECE, 16), 4 * PIECE)
    turned_high, turned_low = halves(block[...].T)
    wide = dot16(jnp.concatenate([turned_high, turned_low], axis=0), high[rows, :], ((1,), (0,)))
    return wide[:WIDTH] + wide[WIDTH:] + dot16(turned_high, low[rows, :], ((1,), (0,)))


def near_kernel(place, high, low, own, front, back, image, gram, gram_near):
    total = jnp.zeros((WIDTH, COLS), F32)
    for k, block in zip(around(place[1]), (own, front, back)):
        total += turned_image(place, k, block, high, low)
    image[...] = total
    gram[...] = full_dot(own[...], own[...], ((0,), (0,)))
    gram_near[...] = full_dot(front[...], front[...], ((0,), (0,))) + full_dot(back[...], back[...], ((0,), (0,)))


def image_kernel(place, whole, high, low, near, gram, gram_near, own, front, back, far, sent, kept, across):
    blocks = (own, front, back, far)
    total = (gram[...] + full_dot(far[...], far[...], ((0,), (0,)))) + gram_near[...]
    for out in (sent, kept):
        out[8 * PIECE : 8 * PIECE + WIDTH, :] = total
        out[8 * PIECE + WIDTH :, :] = jnp.zeros((WIDTH, WIDTH), F32)
    for k, piece in zip(around(place[1]), blocks):

        @pl.when((place[0] == 0) & (place[1] == 0) & (place[2] == k))
        def _(piece=piece):
            kept[8 * PIECE + WIDTH :, :] = piece[:WIDTH, :]
            sent[8 * PIECE + WIDTH :, :] = piece[:WIDTH, :]

    image = (near[...] + turned_image(place, 2, far, high, low)).T
    block, half = 2 * (place[3] % 2) + place[2] // 2, place[2] % 2
    for k, piece in zip(around(place[1]), blocks):

        @pl.when((place[2] - k + 4) % 4 == block)
        def _(piece=piece):
            across[...] = piece[pl.ds(pl.multiple_of(half * 2 * PIECE, 16), 2 * PIECE), :]

    corner = whole[:WIDTH, :].T * jnp.where((place[0] == 0) & (place[1] == 0), 1.0, 0.0)
    for out, half in ((kept, place[1]), (sent, 1 - place[1])):
        for value in range(2):

            @pl.when(half == value)
            def _(out=out, value=value):
                for x in range(4):
                    index = (2 * x + value) * PIECE
                    out[x * PIECE : (x + 1) * PIECE, :] = image[index : index + PIECE, :]
                    out[(4 + x) * PIECE : (5 + x) * PIECE, :] = corner[index : index + PIECE, :]


def factor_kernel(own, r1, r3, r2, upper, upper_here, normal, work):
    total = (own[...] + r2[...]) + (r1[...] + r3[...])
    gram = total[:WIDTH, :]
    work[...] = gram
    cholesky_rows(work, upper_here)
    factor = upper_here[...]
    upper[...] = factor
    normal[...] = gram + full_dot(total[WIDTH:, :], factor, ((0,), (0,)))


def combine_kernel(own, r1, r3, r2, upper, image):
    total = (own[...] + r2[...]) + (r1[...] + r3[...])
    image[...] = total[:PIECE, :] + split_dot(total[PIECE:, :], upper[...], ((1,), (0,)))


def deal_kernel(place, kept, received, small, m0, m1, m3, m2):
    small[...] = kept[8 * PIECE :, :] + received[8 * PIECE :, :]
    for k, out in ((0, m0), (1, m1), (3, m3), (2, m2)):
        for part in range(2):
            start = pl.multiple_of((4 * part + (place[0] + k) % 4) * PIECE, 16)
            rows = pl.ds(start, PIECE)
            out[part * PIECE : (part + 1) * PIECE, :] = kept[rows, :] + received[rows, :]


def untag_kernel(place, p0, p1, p3, p2, out):
    pieces = (p0, p1, p3, p2)
    put_in_order(place[0], ALONG, [p.at[:PIECE, :] for p in pieces], out, PIECE)
    put_in_order(place[0], ALONG, [p.at[PIECE:, :] for p in pieces], out, PIECE, 4 * PIECE)


def cholesky_rows(work, factor):
    lanes = lax.broadcasted_iota(jnp.int32, (1, WIDTH), 1)
    subs = lax.broadcasted_iota(jnp.int32, (8, 1), 0)

    def body(t, carry):
        first = pl.multiple_of(8 * t, 8)
        whole = work[...]
        block = work[pl.ds(first, 8), :]
        columns = [lane(whole, first + b) for b in range(8)]
        pivots = [lane(block, first + b) for b in range(8)]
        for i in range(8):
            row, pivot = block[i : i + 1], pivots[i][i : i + 1]
            inverse = 1.0 / pivot
            scaled = row * lax.rsqrt(pivot)
            factor[pl.ds(first + i, 1), :] = jnp.where(lanes >= first + i, scaled, 0.0)
            column, here = pivots[i], subs == i
            row = row * inverse
            block = jnp.where(here, row, block - column * row)
            for b in range(i + 1, 8):
                entry = pivots[b][i : i + 1] * inverse
                pivots[b] = jnp.where(here, entry, pivots[b] - column * entry)
        for i in range(8):
            whole = whole - columns[i] * block[i : i + 1]
        work[...] = whole
        return carry

    lax.fori_loop(0, WIDTH // 8, body, 0)


def inverse_kernel(source, out):
    out[...] = source[...]
    lanes = lax.broadcasted_iota(jnp.int32, (1, WIDTH), 1)
    subs = lax.broadcasted_iota(jnp.int32, (8, 1), 0)

    def body(t, carry):
        first = pl.multiple_of(8 * t, 8)
        whole = out[...]
        block = out[pl.ds(first, 8), :]
        columns = [lane(whole, first + b) for b in range(8)]
        pivots = [lane(block, first + b) for b in range(8)]
        for i in range(8):
            row, column, here = block[i : i + 1], pivots[i], subs == i
            inverse = 1.0 / column[i : i + 1]
            is_lane = lanes == first + i
            row = jnp.where(is_lane, inverse, row * inverse)
            block = jnp.where(here, row, jnp.where(is_lane, 0.0, block) - column * row)
            for b in range(8):
                if b != i:
                    entry = pivots[b][i : i + 1] * inverse
                    pivots[b] = jnp.where(here, entry, pivots[b] - column * entry)
            pivots[i] = jnp.where(here, inverse, -column * inverse)
        whole = jnp.where((lanes >= first) & (lanes < first + 8), 0.0, whole)
        for i in range(8):
            whole = whole - columns[i] * block[i : i + 1]
        out[...] = whole
        out[pl.ds(first, 8), :] = block
        return carry

    lax.fori_loop(0, WIDTH // 8, body, 0)


def pick_kernel(place, b0, b1, b3, b2, out):
    core, y = place[1], place[3]
    for part in range(2):
        wanted = (y - (2 * (1 - core) + part) + 4) % 4
        for k, block in zip(around(core), (b0, b1, b3, b2)):

            @pl.when(wanted == k)
            def _(block=block, part=part):
                out[part * 4 * PIECE : (part + 1) * 4 * PIECE, :] = block[...]


def gather_kernel(place, p0, p1, p3, p2, upper, b0, b1, b3, b2, swapped, shifted, image_rows, inner):
    x, core, z, y = place[0], place[1], place[2], place[3]
    first = jnp.where((x == 0) & (core == 0), 1.0, 0.0)
    put_in_order(z, around(core), (p0, p1, p3, p2), shifted, 4 * PIECE)
    shifted[:WIDTH, :] += upper[...] * first

    def put(block, offset, part, half):
        for other in range(4):
            start = pl.multiple_of((8 * part + 2 * other + half) * PIECE, 16)
            piece = offset + other * PIECE
            image_rows[pl.ds(start, PIECE), :] = block[piece : piece + PIECE, :]

    for part in range(2):
        wanted = (y - (2 * core + part) + 4) % 4
        for k, block in zip(around(core), (b0, b1, b3, b2)):

            @pl.when(wanted == k)
            def _(block=block, part=part):
                put(block, 0, part, core)

        put(swapped, part * 4 * PIECE, part, 1 - core)
    inner[...] = split_dot(shifted[...], image_rows[...], ((0,), (0,)))


def cols_of(place, own, swapped, target, part):
    for half, block in ((place[1], own), (1 - place[1], swapped)):
        for x in range(4):
            start = pl.multiple_of((2 * x + half) * PIECE, 16)
            piece = (4 * part + x) * PIECE
            target[pl.ds(start, PIECE), :] = block[piece : piece + PIECE, :]


def wide_dot(left, right):
    left_high, left_low = halves(left)
    right_high, right_low = halves(right)
    width = right.shape[1]
    both = dot16(left_high, jnp.concatenate([right_high, right_low], axis=1), ((1,), (0,)))
    return both[:, :width] + both[:, width:] + dot16(left_low, right_high, ((1,), (0,)))


def first_update_kernel(
    place, whole, shifted_rows, image_rows, own, swapped, upper, inverse,
    result, turned, panel_cols, image_cols, right_high, right_low, w_rows,
):
    cols_of(place, own, swapped, image_cols, 0)
    cols_of(place, own, swapped, panel_cols, 1)
    first = jnp.where((place[2] == 0) & (place[3] == 0), 1.0, 0.0)
    panel_cols[:WIDTH, :] += upper[...] * first
    turned[...] = panel_cols[...].T
    w_cols = wide_dot(image_cols[...], inverse[...])
    right_high[:WIDTH, :], right_low[:WIDTH, :] = halves(w_cols.T)
    right_high[WIDTH:, :], right_low[WIDTH:, :] = halves(turned[...])
    w_rows[...] = wide_dot(image_rows[...], inverse[...])
    dims = ((1,), (0,))
    for i in range(ROWS // WIDTH):
        rows = slice(i * WIDTH, (i + 1) * WIDTH)
        left_high, left_low = halves(jnp.concatenate([shifted_rows[rows, :], w_rows[rows, :]], axis=1))
        change = dot16(left_low, right_high[...], dims) + dot16(left_high, right_low[...], dims)
        result[rows, :] = whole[rows, :] - (change + dot16(left_high, right_high[...], dims))


def last_update_kernel(base, shifted_rows, turned, inverse, k0, k1, k3, k2, out, right, right_low, result, sems):
    inner = (k0[...] + k2[...]) + (k1[...] + k3[...])
    dims = ((1,), (0,))
    core_block = split_dot(split_dot(inverse[...], inner, ((0,), (0,))), inverse[...], dims)
    high, low = halves(split_dot(core_block, turned[...], dims))
    right[:WIDTH, :] = high
    right[WIDTH:, :] = high
    right_low[...] = low
    copies = []
    for i in range(ROWS // WIDTH):
        rows = slice(i * WIDTH, (i + 1) * WIDTH)
        left_high, left_low = halves(shifted_rows[rows, :])
        change = dot16(jnp.concatenate([left_high, left_low], axis=1), right[...], dims)
        result[rows, :] = base[rows, :] + (change + dot16(left_high, right_low[...], dims))
        rows = pl.ds(i * WIDTH, WIDTH)
        copies.append(pltpu.make_async_copy(result.at[rows, :], out.at[rows, :], sems.at[i]))
        copies[-1].start()
    for copy in copies:
        copy.wait()


def shape(rows, columns=WIDTH):
    return jax.ShapeDtypeStruct((rows, columns), F32)


def params(mib):
    return pltpu.CompilerParams(vmem_limit_bytes=mib * 1024 * 1024)


def local(kernel, out_shape, mib, scratch=(), flops=0):
    cost = pl.CostEstimate(flops=flops, bytes_accessed=0, transcendentals=0) if flops else None

    def run(*operands):
        specs = [SMEM if value.dtype == jnp.int32 else VMEM for value in operands]
        outs = [VMEM] * len(out_shape) if isinstance(out_shape, list) else VMEM
        return pl.pallas_call(
            kernel, in_specs=specs, out_specs=outs, out_shape=out_shape, scratch_shapes=list(scratch),
            compiler_params=params(mib), cost_estimate=cost,
        )(*operands)

    return run


def turn(axis, first):
    def where(x, core, z, y):
        return axis(first if core == 0 else 4 - first)(x, core, z, y)

    return where


def after(values, *earlier):
    return lax.optimization_barrier((values, earlier))[0]


def shards(panel, trailing):
    row, col = lax.axis_index("row"), lax.axis_index("col")
    place = jnp.stack([row // 2, row % 2, col // 4, col % 4]).astype(jnp.int32)
    anywhere = pl.BlockSpec(memory_space=pl.ANY)
    tile = shape(WIDTH)
    tile16 = jax.ShapeDtypeStruct((ROWS, COLS), BF16)

    with jax.named_scope("panel_y"):
        in_y = local(join_y_kernel, shape(4 * PIECE), 4)(place, panel, *ring(panel, along_y))
    with jax.named_scope("panel_z"):
        below, above = send(in_y, turn(along_z, 1)), send(in_y, turn(along_z, 3))
    with jax.named_scope("split"):
        whole, high, low = pl.pallas_call(
            split_kernel,
            in_specs=[anywhere, VMEM],
            out_specs=[VMEM] * 3,
            out_shape=[shape(ROWS, COLS), tile16, tile16],
            scratch_shapes=[pltpu.SemaphoreType.DMA((STEPS,))],
            compiler_params=params(24),
            cost_estimate=pl.CostEstimate(flops=0, bytes_accessed=4 * ROWS * COLS, transcendentals=0),
        )(trailing, in_y)
    below, above = after((below, above), whole)
    with jax.named_scope("panel_far"):
        far = send(below, turn(along_z, 1))
    with jax.named_scope("near"):
        near, gram, gram_near = local(near_kernel, [shape(WIDTH, COLS), tile, tile], 16, flops=5 * ROWS * COLS * WIDTH)(
            place, high, low, in_y, below, above
        )
    far = after(far, gram)
    in_z = [in_y, below, above, far]

    with jax.named_scope("image"):
        sent, kept, across = local(
            image_kernel, [shape(8 * PIECE + 2 * WIDTH)] * 2 + [shape(2 * PIECE)], 24, flops=2 * ROWS * COLS * WIDTH
        )(place, whole, high, low, near, gram, gram_near, *in_z)
    with jax.named_scope("image_core"):
        received = send(sent, other_core)
    with jax.named_scope("deal"):
        gram, m0, m1, m3, m2 = local(deal_kernel, [shape(2 * WIDTH)] + [shape(2 * PIECE)] * 4, 8)(place, kept, received)
    with jax.named_scope("gram_x"):
        grams = [gram] + ring(gram, along_x)
    with jax.named_scope("image_x"):
        r1, r3, r2 = (send(m, along_x(k)) for m, k in ((m1, 1), (m3, 3), (m2, 2)))
    with jax.named_scope("panel_across"):
        across = send(after(across, grams), planes(0))
    with jax.named_scope("factor"):
        upper, upper_here, normal = local(factor_kernel, [tile] * 3, 4, [pltpu.VMEM((WIDTH, WIDTH), F32)], 2000000000)(
            *grams
        )
    r1, r3, r2, across = after((r1, r3, r2, across), normal)
    with jax.named_scope("image_x"):
        image = local(combine_kernel, shape(PIECE), 4)(m0, r1, r3, r2, upper_here)

    with jax.named_scope("image_planes"):
        planes_in = [send(image, planes(k)) for k in (0, 1, 3, 2)]
    with jax.named_scope("panel_across"):
        handed = send(local(hand_kernel, shape(PIECE), 4)(place, after(across, planes_in[3])), other_core)
    with jax.named_scope("image_planes"):
        in_plane = local(join_z_kernel, shape(4 * PIECE), 4)(place, *after(planes_in, handed))
    with jax.named_scope("image_y"):
        below, above = send(in_plane, turn(along_y, 1)), send(in_plane, turn(along_y, 3))
    with jax.named_scope("image_columns"):
        tagged = local(tag_kernel, shape(2 * PIECE), 4)(place, image, across, handed)
        sides = ring(tagged, along_x)
    with jax.named_scope("inverse"):
        inverse = local(inverse_kernel, tile, 4, flops=2000000000)(after(normal, in_plane))
    below = after(below, inverse, sides[0])
    with jax.named_scope("image_far"):
        opposite = send(below, turn(along_y, 1))
    blocks = [in_plane, below, above, opposite]
    with jax.named_scope("pick"):
        chosen = local(pick_kernel, shape(8 * PIECE), 8)(place, *blocks)
    with jax.named_scope("image_swap"):
        swapped = send(chosen, other_core)
    with jax.named_scope("image_columns"):
        own = local(untag_kernel, shape(8 * PIECE), 8)(place, tagged, *after(sides, chosen))
        other = send(own, other_core)
    with jax.named_scope("gather"):
        shifted, image_rows, inner = local(gather_kernel, [shape(ROWS), shape(ROWS), tile], 16)(
            place, *in_z, upper_here, *blocks, swapped
        )
    with jax.named_scope("inner"):
        inner = inner + send(inner, other_core)
        k1, k3, k2 = ring(inner, along_x)

    with jax.named_scope("first_update"):
        base, turned = local(
            first_update_kernel,
            [shape(ROWS, COLS), shape(WIDTH, COLS)],
            24,
            [
                pltpu.VMEM((COLS, WIDTH), F32),
                pltpu.VMEM((COLS, WIDTH), F32),
                pltpu.VMEM((2 * WIDTH, COLS), BF16),
                pltpu.VMEM((2 * WIDTH, COLS), BF16),
                pltpu.VMEM((ROWS, WIDTH), F32),
            ],
            12 * ROWS * COLS * WIDTH,
        )(place, whole, shifted, image_rows, own, other, upper_here, after(inverse, inner))
    k1, k3, k2 = after((k1, k3, k2), base)
    with jax.named_scope("last_update"):
        updated = pl.pallas_call(
            last_update_kernel,
            in_specs=[VMEM] * 8,
            out_specs=anywhere,
            out_shape=shape(ROWS, COLS),
            scratch_shapes=[
                pltpu.VMEM((2 * WIDTH, COLS), BF16),
                pltpu.VMEM((WIDTH, COLS), BF16),
                pltpu.VMEM((ROWS, COLS), F32),
                pltpu.SemaphoreType.DMA((ROWS // WIDTH,)),
            ],
            compiler_params=params(20),
            cost_estimate=pl.CostEstimate(flops=8 * ROWS * COLS * WIDTH, bytes_accessed=4 * ROWS * COLS, transcendentals=0),
        )(base, shifted, turned, inverse, inner, k1, k3, k2)
    return upper, updated


def solution(mesh):
    return jax.shard_map(
        shards,
        mesh=mesh,
        in_specs=(P(("row", "col"), None), P("row", "col")),
        out_specs=(P(), P("row", "col")),
        check_vma=False,
    )
```

```python
import jax
import jax.numpy as jnp
from jax import lax
from jax.experimental import pallas as pl
from jax.experimental.pallas import tpu as pltpu
from jax.sharding import PartitionSpec as P

F32 = jnp.float32
BF16 = jnp.bfloat16
AXES = ("row", "col")
PIECE = 144
WIDTH = 128
ROWS = 16 * PIECE
COLS = 8 * PIECE
TALL = 256
STEPS = ROWS // TALL
VMEM = pl.BlockSpec(memory_space=pltpu.VMEM)
SMEM = pl.BlockSpec(memory_space=pltpu.SMEM)


def pairs(where):
    result = []
    for x in range(4):
        for core in range(2):
            for z in range(4):
                for y in range(4):
                    tx, tcore, tz, ty = where(x, core, z, y)
                    source = (2 * x + core) * 16 + 4 * z + y
                    target = (2 * tx + tcore) * 16 + 4 * tz + ty
                    result.append((source, target))
    return result


def send(value, where):
    return lax.ppermute(value, AXES, pairs(where))


def along_x(k):
    return lambda x, core, z, y: ((x + k) % 4, core, z, y)


def along_z(k):
    return lambda x, core, z, y: (x, core, (z + k) % 4, y)


def along_y(k):
    return lambda x, core, z, y: (x, core, z, (y + k) % 4)


def other_core(x, core, z, y):
    return (x, 1 - core, z, y)


def planes(k):
    return lambda x, core, z, y: (z, core, (x + k) % 4, y)


def ring(value, direction):
    return [send(value, direction(k)) for k in (1, 3, 2)]


def halves(value):
    high = value.astype(BF16)
    return high, (value - high.astype(F32)).astype(BF16)


def dot16(left, right, dims):
    return lax.dot_general(left, right, (dims, ((), ())), preferred_element_type=F32)


def split_dot(left, right, dims):
    left_high, left_low = halves(left)
    right_high, right_low = halves(right)
    return (
        dot16(left_low, right_high, dims)
        + dot16(left_high, right_low, dims)
        + dot16(left_high, right_high, dims)
    )


def full_dot(left, right, dims=((1,), (0,))):
    return lax.dot_general(
        left, right, (dims, ((), ())), precision=lax.Precision.HIGHEST, preferred_element_type=F32
    )


def lane(value, index):
    return jnp.take_along_axis(value, jnp.full(value.shape, index, jnp.int32), axis=1)


ALONG = (0, 1, 3, 2)


def around(core):
    return (0, 1 + 2 * core, 3 - 2 * core, 2)


def put_in_order(at, steps, pieces, out, rows, first=0):
    for k, piece in zip(steps, pieces):
        start = pl.multiple_of(first + ((at - k + 4) % 4) * rows, 16)
        out[pl.ds(start, rows), :] = piece[...]


def join_y_kernel(place, p0, p1, p3, p2, out):
    put_in_order(place[3], ALONG, (p0, p1, p3, p2), out, PIECE)


def join_z_kernel(place, p0, p1, p3, p2, out):
    put_in_order(place[2], ALONG, (p0, p1, p3, p2), out, PIECE)


def hand_kernel(place, across, out):
    out[...] = across[pl.ds(pl.multiple_of((1 - place[1]) * PIECE, 16), PIECE), :]


def tag_kernel(place, image, across, handed, out):
    out[:PIECE, :] = image[...]

    @pl.when(place[3] // 2 == place[1])
    def _():
        out[PIECE:, :] = across[pl.ds(pl.multiple_of(place[1] * PIECE, 16), PIECE), :]

    @pl.when(place[3] // 2 != place[1])
    def _():
        out[PIECE:, :] = handed[...]


def split_kernel(trailing, after, whole, high, low, sems):
    copies = []
    for i in range(STEPS):
        rows = pl.ds(i * TALL, TALL)
        copies.append(pltpu.make_async_copy(trailing.at[rows, :], whole.at[rows, :], sems.at[i]))
        copies[-1].start()
    for i in range(STEPS):
        copies[i].wait()
        rows = slice(i * TALL, (i + 1) * TALL)
        high[rows, :], low[rows, :] = halves(whole[rows, :])


def turned_image(place, k, block, high, low):
    rows = pl.ds(pl.multiple_of(((place[2] - k + 4) % 4) * 4 * PIECE, 16), 4 * PIECE)
    turned_high, turned_low = halves(block[...].T)
    wide = dot16(jnp.concatenate([turned_high, turned_low], axis=0), high[rows, :], ((1,), (0,)))
    return wide[:WIDTH] + wide[WIDTH:] + dot16(turned_high, low[rows, :], ((1,), (0,)))


def near_kernel(place, high, low, own, front, back, image, gram, gram_near):
    total = jnp.zeros((WIDTH, COLS), F32)
    for k, block in zip(around(place[1]), (own, front, back)):
        total += turned_image(place, k, block, high, low)
    image[...] = total
    gram[...] = full_dot(own[...], own[...], ((0,), (0,)))
    gram_near[...] = full_dot(front[...], front[...], ((0,), (0,))) + full_dot(back[...], back[...], ((0,), (0,)))


def image_kernel(place, whole, high, low, near, gram, gram_near, own, front, back, far, sent, kept, across):
    blocks = (own, front, back, far)
    total = (gram[...] + full_dot(far[...], far[...], ((0,), (0,)))) + gram_near[...]
    for out in (sent, kept):
        out[8 * PIECE : 8 * PIECE + WIDTH, :] = total
        out[8 * PIECE + WIDTH :, :] = jnp.zeros((WIDTH, WIDTH), F32)
    for k, piece in zip(around(place[1]), blocks):

        @pl.when((place[0] == 0) & (place[1] == 0) & (place[2] == k))
        def _(piece=piece):
            kept[8 * PIECE + WIDTH :, :] = piece[:WIDTH, :]
            sent[8 * PIECE + WIDTH :, :] = piece[:WIDTH, :]

    image = (near[...] + turned_image(place, 2, far, high, low)).T
    block, half = 2 * (place[3] % 2) + place[2] // 2, place[2] % 2
    for k, piece in zip(around(place[1]), blocks):

        @pl.when((place[2] - k + 4) % 4 == block)
        def _(piece=piece):
            across[...] = piece[pl.ds(pl.multiple_of(half * 2 * PIECE, 16), 2 * PIECE), :]

    corner = whole[:WIDTH, :].T * jnp.where((place[0] == 0) & (place[1] == 0), 1.0, 0.0)
    for out, half in ((kept, place[1]), (sent, 1 - place[1])):
        for value in range(2):

            @pl.when(half == value)
            def _(out=out, value=value):
                for x in range(4):
                    index = (2 * x + value) * PIECE
                    out[x * PIECE : (x + 1) * PIECE, :] = image[index : index + PIECE, :]
                    out[(4 + x) * PIECE : (5 + x) * PIECE, :] = corner[index : index + PIECE, :]


def factor_kernel(own, r1, r3, r2, gram, upper, upper_here, work):
    total = (own[...] + r2[...]) + (r1[...] + r3[...])
    gram[...] = total
    work[...] = total
    cholesky_rows(work, upper_here)
    upper[...] = upper_here[...]


def combine_kernel(own, r1, r3, r2, gram, upper, image, normal):
    total = (own[...] + r2[...]) + (r1[...] + r3[...])
    image[...] = total[:PIECE, :] + split_dot(total[PIECE : 2 * PIECE, :], upper[...], ((1,), (0,)))
    normal[...] = gram[...] + full_dot(total[2 * PIECE :, :], upper[...], ((0,), (0,)))


def deal_kernel(place, kept, received, small, m0, m1, m3, m2):
    small[...] = kept[8 * PIECE : 8 * PIECE + WIDTH, :] + received[8 * PIECE : 8 * PIECE + WIDTH, :]
    top = kept[8 * PIECE + WIDTH :, :] + received[8 * PIECE + WIDTH :, :]
    for k, out in ((0, m0), (1, m1), (3, m3), (2, m2)):
        for part in range(2):
            start = pl.multiple_of((4 * part + (place[0] + k) % 4) * PIECE, 16)
            rows = pl.ds(start, PIECE)
            out[part * PIECE : (part + 1) * PIECE, :] = kept[rows, :] + received[rows, :]
        out[2 * PIECE :, :] = top


def untag_kernel(place, p0, p1, p3, p2, out):
    pieces = (p0, p1, p3, p2)
    put_in_order(place[0], ALONG, [p.at[:PIECE, :] for p in pieces], out, PIECE)
    put_in_order(place[0], ALONG, [p.at[PIECE:, :] for p in pieces], out, PIECE, 4 * PIECE)


def cholesky_rows(work, factor):
    lanes = lax.broadcasted_iota(jnp.int32, (1, WIDTH), 1)
    subs = lax.broadcasted_iota(jnp.int32, (8, 1), 0)

    def body(t, carry):
        first = pl.multiple_of(8 * t, 8)
        whole = work[...]
        block = work[pl.ds(first, 8), :]
        columns = [lane(whole, first + b) for b in range(8)]
        pivots = [lane(block, first + b) for b in range(8)]
        for i in range(8):
            row, pivot = block[i : i + 1], pivots[i][i : i + 1]
            inverse = 1.0 / pivot
            scaled = row * lax.rsqrt(pivot)
            factor[pl.ds(first + i, 1), :] = jnp.where(lanes >= first + i, scaled, 0.0)
            column, here = pivots[i], subs == i
            row = row * inverse
            block = jnp.where(here, row, block - column * row)
            for b in range(i + 1, 8):
                entry = pivots[b][i : i + 1] * inverse
                pivots[b] = jnp.where(here, entry, pivots[b] - column * entry)
        for i in range(8):
            whole = whole - columns[i] * block[i : i + 1]
        work[...] = whole
        return carry

    lax.fori_loop(0, WIDTH // 8, body, 0)


def inverse_kernel(source, out):
    out[...] = source[...]
    lanes = lax.broadcasted_iota(jnp.int32, (1, WIDTH), 1)
    subs = lax.broadcasted_iota(jnp.int32, (8, 1), 0)

    def body(t, carry):
        first = pl.multiple_of(8 * t, 8)
        whole = out[...]
        block = out[pl.ds(first, 8), :]
        columns = [lane(whole, first + b) for b in range(8)]
        pivots = [lane(block, first + b) for b in range(8)]
        for i in range(8):
            row, column, here = block[i : i + 1], pivots[i], subs == i
            inverse = 1.0 / column[i : i + 1]
            is_lane = lanes == first + i
            row = jnp.where(is_lane, inverse, row * inverse)
            block = jnp.where(here, row, jnp.where(is_lane, 0.0, block) - column * row)
            for b in range(8):
                if b != i:
                    entry = pivots[b][i : i + 1] * inverse
                    pivots[b] = jnp.where(here, entry, pivots[b] - column * entry)
            pivots[i] = jnp.where(here, inverse, -column * inverse)
        whole = jnp.where((lanes >= first) & (lanes < first + 8), 0.0, whole)
        for i in range(8):
            whole = whole - columns[i] * block[i : i + 1]
        out[...] = whole
        out[pl.ds(first, 8), :] = block
        return carry

    lax.fori_loop(0, WIDTH // 8, body, 0)


def pick_kernel(place, b0, b1, b3, b2, out):
    core, y = place[1], place[3]
    for part in range(2):
        wanted = (y - (2 * (1 - core) + part) + 4) % 4
        for k, block in zip(around(core), (b0, b1, b3, b2)):

            @pl.when(wanted == k)
            def _(block=block, part=part):
                out[part * 4 * PIECE : (part + 1) * 4 * PIECE, :] = block[...]


def gather_kernel(place, p0, p1, p3, p2, upper, b0, b1, b3, b2, swapped, shifted, image_rows, inner):
    x, core, z, y = place[0], place[1], place[2], place[3]
    first = jnp.where((x == 0) & (core == 0), 1.0, 0.0)
    put_in_order(z, around(core), (p0, p1, p3, p2), shifted, 4 * PIECE)
    shifted[:WIDTH, :] += upper[...] * first

    def put(block, offset, part, half):
        for other in range(4):
            start = pl.multiple_of((8 * part + 2 * other + half) * PIECE, 16)
            piece = offset + other * PIECE
            image_rows[pl.ds(start, PIECE), :] = block[piece : piece + PIECE, :]

    for part in range(2):
        wanted = (y - (2 * core + part) + 4) % 4
        for k, block in zip(around(core), (b0, b1, b3, b2)):

            @pl.when(wanted == k)
            def _(block=block, part=part):
                put(block, 0, part, core)

        put(swapped, part * 4 * PIECE, part, 1 - core)
    inner[...] = split_dot(shifted[...], image_rows[...], ((0,), (0,)))


def cols_of(place, own, swapped, target, part):
    for half, block in ((place[1], own), (1 - place[1], swapped)):
        for x in range(4):
            start = pl.multiple_of((2 * x + half) * PIECE, 16)
            piece = (4 * part + x) * PIECE
            target[pl.ds(start, PIECE), :] = block[piece : piece + PIECE, :]


def wide_dot(left, right):
    left_high, left_low = halves(left)
    right_high, right_low = halves(right)
    width = right.shape[1]
    both = dot16(left_high, jnp.concatenate([right_high, right_low], axis=1), ((1,), (0,)))
    return both[:, :width] + both[:, width:] + dot16(left_low, right_high, ((1,), (0,)))


def first_update_kernel(
    place, whole, shifted_rows, image_rows, own, swapped, upper, inverse,
    result, turned, panel_cols, image_cols, right_high, right_low, w_rows,
):
    cols_of(place, own, swapped, image_cols, 0)
    cols_of(place, own, swapped, panel_cols, 1)
    first = jnp.where((place[2] == 0) & (place[3] == 0), 1.0, 0.0)
    panel_cols[:WIDTH, :] += upper[...] * first
    turned[...] = panel_cols[...].T
    w_cols = wide_dot(image_cols[...], inverse[...])
    right_high[:WIDTH, :], right_low[:WIDTH, :] = halves(w_cols.T)
    right_high[WIDTH:, :], right_low[WIDTH:, :] = halves(turned[...])
    w_rows[...] = wide_dot(image_rows[...], inverse[...])
    dims = ((1,), (0,))
    for i in range(ROWS // WIDTH):
        rows = slice(i * WIDTH, (i + 1) * WIDTH)
        left_high, left_low = halves(jnp.concatenate([shifted_rows[rows, :], w_rows[rows, :]], axis=1))
        change = dot16(left_low, right_high[...], dims) + dot16(left_high, right_low[...], dims)
        result[rows, :] = whole[rows, :] - (change + dot16(left_high, right_high[...], dims))


def last_update_kernel(base, shifted_rows, turned, inverse, k0, k1, k3, k2, out, right, right_low, result, sems):
    inner = (k0[...] + k2[...]) + (k1[...] + k3[...])
    dims = ((1,), (0,))
    core_block = split_dot(split_dot(inverse[...], inner, ((0,), (0,))), inverse[...], dims)
    high, low = halves(split_dot(core_block, turned[...], dims))
    right[:WIDTH, :] = high
    right[WIDTH:, :] = high
    right_low[...] = low
    copies = []
    for i in range(ROWS // WIDTH):
        rows = slice(i * WIDTH, (i + 1) * WIDTH)
        left_high, left_low = halves(shifted_rows[rows, :])
        change = dot16(jnp.concatenate([left_high, left_low], axis=1), right[...], dims)
        result[rows, :] = base[rows, :] + (change + dot16(left_high, right_low[...], dims))
        rows = pl.ds(i * WIDTH, WIDTH)
        copies.append(pltpu.make_async_copy(result.at[rows, :], out.at[rows, :], sems.at[i]))
        copies[-1].start()
    for copy in copies:
        copy.wait()


def shape(rows, columns=WIDTH):
    return jax.ShapeDtypeStruct((rows, columns), F32)


def params(mib):
    return pltpu.CompilerParams(vmem_limit_bytes=mib * 1024 * 1024)


def local(kernel, out_shape, mib, scratch=(), flops=0):
    cost = pl.CostEstimate(flops=flops, bytes_accessed=0, transcendentals=0) if flops else None

    def run(*operands):
        specs = [SMEM if value.dtype == jnp.int32 else VMEM for value in operands]
        outs = [VMEM] * len(out_shape) if isinstance(out_shape, list) else VMEM
        return pl.pallas_call(
            kernel, in_specs=specs, out_specs=outs, out_shape=out_shape, scratch_shapes=list(scratch),
            compiler_params=params(mib), cost_estimate=cost,
        )(*operands)

    return run


def turn(axis, first):
    def where(x, core, z, y):
        return axis(first if core == 0 else 4 - first)(x, core, z, y)

    return where


def after(values, *earlier):
    return lax.optimization_barrier((values, earlier))[0]


def shards(panel, trailing):
    row, col = lax.axis_index("row"), lax.axis_index("col")
    place = jnp.stack([row // 2, row % 2, col // 4, col % 4]).astype(jnp.int32)
    anywhere = pl.BlockSpec(memory_space=pl.ANY)
    tile = shape(WIDTH)
    tile16 = jax.ShapeDtypeStruct((ROWS, COLS), BF16)

    with jax.named_scope("panel_y"):
        in_y = local(join_y_kernel, shape(4 * PIECE), 4)(place, panel, *ring(panel, along_y))
    with jax.named_scope("panel_z"):
        below, above = send(in_y, turn(along_z, 1)), send(in_y, turn(along_z, 3))
    with jax.named_scope("split"):
        whole, high, low = pl.pallas_call(
            split_kernel,
            in_specs=[anywhere, VMEM],
            out_specs=[VMEM] * 3,
            out_shape=[shape(ROWS, COLS), tile16, tile16],
            scratch_shapes=[pltpu.SemaphoreType.DMA((STEPS,))],
            compiler_params=params(24),
            cost_estimate=pl.CostEstimate(flops=0, bytes_accessed=4 * ROWS * COLS, transcendentals=0),
        )(trailing, in_y)
    below, above = after((below, above), whole)
    with jax.named_scope("panel_far"):
        far = send(below, turn(along_z, 1))
    with jax.named_scope("near"):
        near, gram, gram_near = local(near_kernel, [shape(WIDTH, COLS), tile, tile], 16, flops=5 * ROWS * COLS * WIDTH)(
            place, high, low, in_y, below, above
        )
    far = after(far, gram)
    in_z = [in_y, below, above, far]

    with jax.named_scope("image"):
        sent, kept, across = local(
            image_kernel, [shape(8 * PIECE + 2 * WIDTH)] * 2 + [shape(2 * PIECE)], 24, flops=2 * ROWS * COLS * WIDTH
        )(place, whole, high, low, near, gram, gram_near, *in_z)
    with jax.named_scope("image_core"):
        received = send(sent, other_core)
    with jax.named_scope("deal"):
        gram, m0, m1, m3, m2 = local(deal_kernel, [tile] + [shape(2 * PIECE + WIDTH)] * 4, 8)(place, kept, received)
    with jax.named_scope("gram_x"):
        grams = [gram] + ring(gram, along_x)
    with jax.named_scope("image_x"):
        r1, r3, r2 = (send(m, along_x(k)) for m, k in ((m1, 1), (m3, 3), (m2, 2)))
    with jax.named_scope("panel_across"):
        across = send(after(across, grams), planes(0))
    with jax.named_scope("factor"):
        gram, upper, upper_here = local(factor_kernel, [tile] * 3, 4, [pltpu.VMEM((WIDTH, WIDTH), F32)], 2000000000)(
            *grams
        )
    r1, r3, r2 = after((r1, r3, r2), upper_here)
    with jax.named_scope("image_x"):
        image, normal = local(combine_kernel, [shape(PIECE), tile], 4)(m0, r1, r3, r2, gram, upper_here)

    with jax.named_scope("image_planes"):
        planes_in = [send(image, planes(k)) for k in (0, 1, 3, 2)]
    with jax.named_scope("panel_across"):
        handed = send(local(hand_kernel, shape(PIECE), 4)(place, after(across, planes_in[3])), other_core)
    with jax.named_scope("image_planes"):
        in_plane = local(join_z_kernel, shape(4 * PIECE), 4)(place, *after(planes_in, handed))
    with jax.named_scope("image_y"):
        below, above = send(in_plane, turn(along_y, 1)), send(in_plane, turn(along_y, 3))
    with jax.named_scope("image_columns"):
        tagged = local(tag_kernel, shape(2 * PIECE), 4)(place, image, across, handed)
        sides = ring(tagged, along_x)
    with jax.named_scope("inverse"):
        inverse = local(inverse_kernel, tile, 4, flops=2000000000)(after(normal, in_plane))
    below = after(below, inverse, sides[0])
    with jax.named_scope("image_far"):
        opposite = send(below, turn(along_y, 1))
    blocks = [in_plane, below, above, opposite]
    with jax.named_scope("pick"):
        chosen = local(pick_kernel, shape(8 * PIECE), 8)(place, *blocks)
    with jax.named_scope("image_swap"):
        swapped = send(chosen, other_core)
    with jax.named_scope("image_columns"):
        own = local(untag_kernel, shape(8 * PIECE), 8)(place, tagged, *after(sides, chosen))
        other = send(own, other_core)
    with jax.named_scope("gather"):
        shifted, image_rows, inner = local(gather_kernel, [shape(ROWS), shape(ROWS), tile], 16)(
            place, *in_z, upper_here, *blocks, swapped
        )
    with jax.named_scope("inner"):
        inner = inner + send(inner, other_core)
        k1, k3, k2 = ring(inner, along_x)

    with jax.named_scope("first_update"):
        base, turned = local(
            first_update_kernel,
            [shape(ROWS, COLS), shape(WIDTH, COLS)],
            24,
            [
                pltpu.VMEM((COLS, WIDTH), F32),
                pltpu.VMEM((COLS, WIDTH), F32),
                pltpu.VMEM((2 * WIDTH, COLS), BF16),
                pltpu.VMEM((2 * WIDTH, COLS), BF16),
                pltpu.VMEM((ROWS, WIDTH), F32),
            ],
            12 * ROWS * COLS * WIDTH,
        )(place, whole, shifted, image_rows, own, other, upper_here, after(inverse, inner))
    k1, k3, k2 = after((k1, k3, k2), base)
    with jax.named_scope("last_update"):
        updated = pl.pallas_call(
            last_update_kernel,
            in_specs=[VMEM] * 8,
            out_specs=anywhere,
            out_shape=shape(ROWS, COLS),
            scratch_shapes=[
                pltpu.VMEM((2 * WIDTH, COLS), BF16),
                pltpu.VMEM((WIDTH, COLS), BF16),
                pltpu.VMEM((ROWS, COLS), F32),
                pltpu.SemaphoreType.DMA((ROWS // WIDTH,)),
            ],
            compiler_params=params(20),
            cost_estimate=pl.CostEstimate(flops=8 * ROWS * COLS * WIDTH, bytes_accessed=4 * ROWS * COLS, transcendentals=0),
        )(base, shifted, turned, inverse, inner, k1, k3, k2)
    return upper, updated


def solution(mesh):
    return jax.shard_map(
        shards,
        mesh=mesh,
        in_specs=(P(("row", "col"), None), P("row", "col")),
        out_specs=(P(), P("row", "col")),
        check_vma=False,
    )
```

```python
import jax
import jax.numpy as jnp
from jax import lax
from jax.experimental import pallas as pl
from jax.experimental.pallas import tpu as pltpu
from jax.sharding import PartitionSpec as P

F32 = jnp.float32
BF16 = jnp.bfloat16
AXES = ("row", "col")
PIECE = 144
WIDTH = 128
ROWS = 16 * PIECE
COLS = 8 * PIECE
TALL = 256
STEPS = ROWS // TALL
VMEM = pl.BlockSpec(memory_space=pltpu.VMEM)
SMEM = pl.BlockSpec(memory_space=pltpu.SMEM)


def pairs(where, only=None):
    result = []
    for x in range(4):
        for core in range(2):
            for z in range(4):
                for y in range(4):
                    if only is not None and not only(x, core, z, y):
                        continue
                    tx, tcore, tz, ty = where(x, core, z, y)
                    source = (2 * x + core) * 16 + 4 * z + y
                    target = (2 * tx + tcore) * 16 + 4 * tz + ty
                    result.append((source, target))
    return result


def send(value, where, only=None):
    return lax.ppermute(value, AXES, pairs(where, only))


def along_x(k):
    return lambda x, core, z, y: ((x + k) % 4, core, z, y)


def along_z(k):
    return lambda x, core, z, y: (x, core, (z + k) % 4, y)


def along_y(k):
    return lambda x, core, z, y: (x, core, z, (y + k) % 4)


def other_core(x, core, z, y):
    return (x, 1 - core, z, y)


def planes(k):
    return lambda x, core, z, y: (z, core, (x + k) % 4, y)


def ring(value, direction):
    return [send(value, direction(k)) for k in (1, 3, 2)]


def halves(value):
    high = value.astype(BF16)
    return high, (value - high.astype(F32)).astype(BF16)


def dot16(left, right, dims):
    return lax.dot_general(left, right, (dims, ((), ())), preferred_element_type=F32)


def split_dot(left, right, dims):
    left_high, left_low = halves(left)
    right_high, right_low = halves(right)
    return (
        dot16(left_low, right_high, dims)
        + dot16(left_high, right_low, dims)
        + dot16(left_high, right_high, dims)
    )


def full_dot(left, right, dims=((1,), (0,))):
    return lax.dot_general(
        left, right, (dims, ((), ())), precision=lax.Precision.HIGHEST, preferred_element_type=F32
    )


def lane(value, index):
    return jnp.take_along_axis(value, jnp.full(value.shape, index, jnp.int32), axis=1)


ALONG = (0, 1, 3, 2)


def around(core):
    return (0, 1 + 2 * core, 3 - 2 * core, 2)


def put_in_order(at, steps, pieces, out, rows, first=0):
    for k, piece in zip(steps, pieces):
        start = pl.multiple_of(first + ((at - k + 4) % 4) * rows, 16)
        out[pl.ds(start, rows), :] = piece[...]


def join_y_kernel(place, p0, p1, p3, p2, out):
    put_in_order(place[3], ALONG, (p0, p1, p3, p2), out, PIECE)


def join_z_kernel(place, p0, p1, p3, p2, out):
    put_in_order(place[2], ALONG, (p0, p1, p3, p2), out, PIECE)


def hand_kernel(place, across, out):
    out[...] = across[pl.ds(pl.multiple_of((1 - place[1]) * PIECE, 16), PIECE), :]


def tag_kernel(place, image, across, handed, out):
    out[:PIECE, :] = image[...]

    @pl.when(place[3] // 2 == place[1])
    def _():
        out[PIECE:, :] = across[pl.ds(pl.multiple_of(place[1] * PIECE, 16), PIECE), :]

    @pl.when(place[3] // 2 != place[1])
    def _():
        out[PIECE:, :] = handed[...]


def split_kernel(trailing, after, whole, high, low, sems):
    copies = []
    for i in range(STEPS):
        rows = pl.ds(i * TALL, TALL)
        copies.append(pltpu.make_async_copy(trailing.at[rows, :], whole.at[rows, :], sems.at[i]))
        copies[-1].start()
    for i in range(STEPS):
        copies[i].wait()
        rows = slice(i * TALL, (i + 1) * TALL)
        high[rows, :], low[rows, :] = halves(whole[rows, :])


def turned_image(place, k, block, high, low):
    rows = pl.ds(pl.multiple_of(((place[2] - k + 4) % 4) * 4 * PIECE, 16), 4 * PIECE)
    turned_high, turned_low = halves(block[...].T)
    wide = dot16(jnp.concatenate([turned_high, turned_low], axis=0), high[rows, :], ((1,), (0,)))
    return wide[:WIDTH] + wide[WIDTH:] + dot16(turned_high, low[rows, :], ((1,), (0,)))


def near_kernel(place, high, low, own, front, back, image, gram, gram_near):
    total = jnp.zeros((WIDTH, COLS), F32)
    for k, block in zip(around(place[1]), (own, front, back)):
        total += turned_image(place, k, block, high, low)
    image[...] = total
    gram[...] = full_dot(own[...], own[...], ((0,), (0,)))
    gram_near[...] = full_dot(front[...], front[...], ((0,), (0,))) + full_dot(back[...], back[...], ((0,), (0,)))


def image_kernel(place, whole, high, low, near, gram, gram_near, own, front, back, far, sent, kept, across):
    blocks = (own, front, back, far)
    total = (gram[...] + full_dot(far[...], far[...], ((0,), (0,)))) + gram_near[...]
    for out in (sent, kept):
        out[8 * PIECE : 8 * PIECE + WIDTH, :] = total
        out[8 * PIECE + WIDTH :, :] = jnp.zeros((WIDTH, WIDTH), F32)
    for k, piece in zip(around(place[1]), blocks):

        @pl.when((place[0] == 0) & (place[1] == 0) & (place[2] == k))
        def _(piece=piece):
            kept[8 * PIECE + WIDTH :, :] = piece[:WIDTH, :]
            sent[8 * PIECE + WIDTH :, :] = piece[:WIDTH, :]

    image = (near[...] + turned_image(place, 2, far, high, low)).T
    block, half = 2 * (place[3] % 2) + place[2] // 2, place[2] % 2
    for k, piece in zip(around(place[1]), blocks):

        @pl.when((place[2] - k + 4) % 4 == block)
        def _(piece=piece):
            across[...] = piece[pl.ds(pl.multiple_of(half * 2 * PIECE, 16), 2 * PIECE), :]

    corner = whole[:WIDTH, :].T * jnp.where((place[0] == 0) & (place[1] == 0), 1.0, 0.0)
    for out, half in ((kept, place[1]), (sent, 1 - place[1])):
        for value in range(2):

            @pl.when(half == value)
            def _(out=out, value=value):
                for x in range(4):
                    index = (2 * x + value) * PIECE
                    out[x * PIECE : (x + 1) * PIECE, :] = image[index : index + PIECE, :]
                    out[(4 + x) * PIECE : (5 + x) * PIECE, :] = corner[index : index + PIECE, :]


def factor_kernel(own, r1, r3, r2, gram, upper, upper_here, work):
    total = (own[...] + r2[...]) + (r1[...] + r3[...])
    gram[...] = total
    work[...] = total
    cholesky_rows(work, upper_here)
    upper[...] = upper_here[...]


def combine_kernel(own, r1, r3, r2, gram, upper, image, normal):
    total = (own[...] + r2[...]) + (r1[...] + r3[...])
    image[...] = total[:PIECE, :] + split_dot(total[PIECE : 2 * PIECE, :], upper[...], ((1,), (0,)))
    normal[...] = gram[...] + full_dot(total[2 * PIECE :, :], upper[...], ((0,), (0,)))


def deal_kernel(place, kept, received, small, m0, m1, m3, m2):
    small[...] = kept[8 * PIECE : 8 * PIECE + WIDTH, :] + received[8 * PIECE : 8 * PIECE + WIDTH, :]
    top = kept[8 * PIECE + WIDTH :, :] + received[8 * PIECE + WIDTH :, :]
    for k, out in ((0, m0), (1, m1), (3, m3), (2, m2)):
        for part in range(2):
            start = pl.multiple_of((4 * part + (place[0] + k) % 4) * PIECE, 16)
            rows = pl.ds(start, PIECE)
            out[part * PIECE : (part + 1) * PIECE, :] = kept[rows, :] + received[rows, :]
        out[2 * PIECE :, :] = top


def untag_kernel(place, p0, p1, p3, p2, out):
    pieces = (p0, p1, p3, p2)
    put_in_order(place[0], ALONG, [p.at[:PIECE, :] for p in pieces], out, PIECE)
    put_in_order(place[0], ALONG, [p.at[PIECE:, :] for p in pieces], out, PIECE, 4 * PIECE)


def cholesky_rows(work, factor):
    lanes = lax.broadcasted_iota(jnp.int32, (1, WIDTH), 1)
    subs = lax.broadcasted_iota(jnp.int32, (8, 1), 0)

    def body(t, carry):
        first = pl.multiple_of(8 * t, 8)
        whole = work[...]
        block = work[pl.ds(first, 8), :]
        columns = [lane(whole, first + b) for b in range(8)]
        pivots = [lane(block, first + b) for b in range(8)]
        for i in range(8):
            row, pivot = block[i : i + 1], pivots[i][i : i + 1]
            inverse = 1.0 / pivot
            scaled = row * lax.rsqrt(pivot)
            factor[pl.ds(first + i, 1), :] = jnp.where(lanes >= first + i, scaled, 0.0)
            column, here = pivots[i], subs == i
            row = row * inverse
            block = jnp.where(here, row, block - column * row)
            for b in range(i + 1, 8):
                entry = pivots[b][i : i + 1] * inverse
                pivots[b] = jnp.where(here, entry, pivots[b] - column * entry)
        for i in range(8):
            whole = whole - columns[i] * block[i : i + 1]
        work[...] = whole
        return carry

    lax.fori_loop(0, WIDTH // 8, body, 0)


def inverse_kernel(source, out):
    out[...] = source[...]
    lanes = lax.broadcasted_iota(jnp.int32, (1, WIDTH), 1)
    subs = lax.broadcasted_iota(jnp.int32, (8, 1), 0)

    def body(t, carry):
        first = pl.multiple_of(8 * t, 8)
        whole = out[...]
        block = out[pl.ds(first, 8), :]
        columns = [lane(whole, first + b) for b in range(8)]
        pivots = [lane(block, first + b) for b in range(8)]
        for i in range(8):
            row, column, here = block[i : i + 1], pivots[i], subs == i
            inverse = 1.0 / column[i : i + 1]
            is_lane = lanes == first + i
            row = jnp.where(is_lane, inverse, row * inverse)
            block = jnp.where(here, row, jnp.where(is_lane, 0.0, block) - column * row)
            for b in range(8):
                if b != i:
                    entry = pivots[b][i : i + 1] * inverse
                    pivots[b] = jnp.where(here, entry, pivots[b] - column * entry)
            pivots[i] = jnp.where(here, inverse, -column * inverse)
        whole = jnp.where((lanes >= first) & (lanes < first + 8), 0.0, whole)
        for i in range(8):
            whole = whole - columns[i] * block[i : i + 1]
        out[...] = whole
        out[pl.ds(first, 8), :] = block
        return carry

    lax.fori_loop(0, WIDTH // 8, body, 0)


def pick_kernel(place, b0, b1, b3, b2, out):
    core, y = place[1], place[3]
    for part in range(2):
        wanted = (y - (2 * (1 - core) + part) + 4) % 4
        for k, block in zip(around(core), (b0, b1, b3, b2)):

            @pl.when(wanted == k)
            def _(block=block, part=part):
                out[part * 4 * PIECE : (part + 1) * 4 * PIECE, :] = block[...]


def gather_kernel(place, p0, p1, p3, p2, upper, b0, b1, b3, b2, swapped, shifted, image_rows, inner):
    x, core, z, y = place[0], place[1], place[2], place[3]
    first = jnp.where((x == 0) & (core == 0), 1.0, 0.0)
    put_in_order(z, around(core), (p0, p1, p3, p2), shifted, 4 * PIECE)
    shifted[:WIDTH, :] += upper[...] * first

    def put(block, offset, part, half):
        for other in range(4):
            start = pl.multiple_of((8 * part + 2 * other + half) * PIECE, 16)
            piece = offset + other * PIECE
            image_rows[pl.ds(start, PIECE), :] = block[piece : piece + PIECE, :]

    for part in range(2):
        wanted = (y - (2 * core + part) + 4) % 4
        for k, block in zip(around(core), (b0, b1, b3, b2)):

            @pl.when(wanted == k)
            def _(block=block, part=part):
                put(block, 0, part, core)

        put(swapped, part * 4 * PIECE, part, 1 - core)
    inner[...] = split_dot(shifted[...], image_rows[...], ((0,), (0,)))


def cols_of(place, own, swapped, target, part):
    for half, block in ((place[1], own), (1 - place[1], swapped)):
        for x in range(4):
            start = pl.multiple_of((2 * x + half) * PIECE, 16)
            piece = (4 * part + x) * PIECE
            target[pl.ds(start, PIECE), :] = block[piece : piece + PIECE, :]


def wide_dot(left, right):
    left_high, left_low = halves(left)
    right_high, right_low = halves(right)
    width = right.shape[1]
    both = dot16(left_high, jnp.concatenate([right_high, right_low], axis=1), ((1,), (0,)))
    return both[:, :width] + both[:, width:] + dot16(left_low, right_high, ((1,), (0,)))


def first_update_kernel(
    place, whole, shifted_rows, image_rows, own, swapped, upper, inverse,
    result, turned, panel_cols, image_cols, right_high, right_low, w_rows,
):
    cols_of(place, own, swapped, image_cols, 0)
    cols_of(place, own, swapped, panel_cols, 1)
    first = jnp.where((place[2] == 0) & (place[3] == 0), 1.0, 0.0)
    panel_cols[:WIDTH, :] += upper[...] * first
    turned[...] = panel_cols[...].T
    w_cols = wide_dot(image_cols[...], inverse[...])
    right_high[:WIDTH, :], right_low[:WIDTH, :] = halves(w_cols.T)
    right_high[WIDTH:, :], right_low[WIDTH:, :] = halves(turned[...])
    w_rows[...] = wide_dot(image_rows[...], inverse[...])
    dims = ((1,), (0,))
    for i in range(ROWS // WIDTH):
        rows = slice(i * WIDTH, (i + 1) * WIDTH)
        left_high, left_low = halves(jnp.concatenate([shifted_rows[rows, :], w_rows[rows, :]], axis=1))
        change = dot16(left_low, right_high[...], dims) + dot16(left_high, right_low[...], dims)
        result[rows, :] = whole[rows, :] - (change + dot16(left_high, right_high[...], dims))


def last_update_kernel(base, shifted_rows, turned, inverse, k0, k1, k3, k2, out, right, right_low, result, sems):
    inner = (k0[...] + k2[...]) + (k1[...] + k3[...])
    dims = ((1,), (0,))
    core_block = split_dot(split_dot(inverse[...], inner, ((0,), (0,))), inverse[...], dims)
    high, low = halves(split_dot(core_block, turned[...], dims))
    right[:WIDTH, :] = high
    right[WIDTH:, :] = high
    right_low[...] = low
    copies = []
    for i in range(ROWS // WIDTH):
        rows = slice(i * WIDTH, (i + 1) * WIDTH)
        left_high, left_low = halves(shifted_rows[rows, :])
        change = dot16(jnp.concatenate([left_high, left_low], axis=1), right[...], dims)
        result[rows, :] = base[rows, :] + (change + dot16(left_high, right_low[...], dims))
        rows = pl.ds(i * WIDTH, WIDTH)
        copies.append(pltpu.make_async_copy(result.at[rows, :], out.at[rows, :], sems.at[i]))
        copies[-1].start()
    for copy in copies:
        copy.wait()


def shape(rows, columns=WIDTH):
    return jax.ShapeDtypeStruct((rows, columns), F32)


def params(mib):
    return pltpu.CompilerParams(vmem_limit_bytes=mib * 1024 * 1024)


def local(kernel, out_shape, mib, scratch=(), flops=0):
    cost = pl.CostEstimate(flops=flops, bytes_accessed=0, transcendentals=0) if flops else None

    def run(*operands):
        specs = [SMEM if value.dtype == jnp.int32 else VMEM for value in operands]
        outs = [VMEM] * len(out_shape) if isinstance(out_shape, list) else VMEM
        return pl.pallas_call(
            kernel, in_specs=specs, out_specs=outs, out_shape=out_shape, scratch_shapes=list(scratch),
            compiler_params=params(mib), cost_estimate=cost,
        )(*operands)

    return run


def turn(axis, first):
    def where(x, core, z, y):
        return axis(first if core == 0 else 4 - first)(x, core, z, y)

    return where


def after(values, *earlier):
    return lax.optimization_barrier((values, earlier))[0]


def shards(panel, trailing):
    row, col = lax.axis_index("row"), lax.axis_index("col")
    place = jnp.stack([row // 2, row % 2, col // 4, col % 4]).astype(jnp.int32)
    anywhere = pl.BlockSpec(memory_space=pl.ANY)
    tile = shape(WIDTH)
    tile16 = jax.ShapeDtypeStruct((ROWS, COLS), BF16)

    with jax.named_scope("panel_y"):
        in_y = local(join_y_kernel, shape(4 * PIECE), 4)(place, panel, *ring(panel, along_y))
    with jax.named_scope("panel_z"):
        below, above = send(in_y, turn(along_z, 1)), send(in_y, turn(along_z, 3))
    with jax.named_scope("split"):
        whole, high, low = pl.pallas_call(
            split_kernel,
            in_specs=[anywhere, VMEM],
            out_specs=[VMEM] * 3,
            out_shape=[shape(ROWS, COLS), tile16, tile16],
            scratch_shapes=[pltpu.SemaphoreType.DMA((STEPS,))],
            compiler_params=params(24),
            cost_estimate=pl.CostEstimate(flops=0, bytes_accessed=4 * ROWS * COLS, transcendentals=0),
        )(trailing, in_y)
    below, above = after((below, above), whole)
    with jax.named_scope("panel_far"):
        far = send(below, turn(along_z, 1))
    with jax.named_scope("near"):
        near, gram, gram_near = local(near_kernel, [shape(WIDTH, COLS), tile, tile], 16, flops=5 * ROWS * COLS * WIDTH)(
            place, high, low, in_y, below, above
        )
    far = after(far, gram)
    in_z = [in_y, below, above, far]

    with jax.named_scope("image"):
        sent, kept, across = local(
            image_kernel, [shape(8 * PIECE + 2 * WIDTH)] * 2 + [shape(2 * PIECE)], 24, flops=2 * ROWS * COLS * WIDTH
        )(place, whole, high, low, near, gram, gram_near, *in_z)
    with jax.named_scope("image_core"):
        received = send(sent, other_core)
    with jax.named_scope("deal"):
        gram, m0, m1, m3, m2 = local(deal_kernel, [tile] + [shape(2 * PIECE + WIDTH)] * 4, 8)(place, kept, received)
    with jax.named_scope("gram_x"):
        grams = [gram] + ring(gram, along_x)
    with jax.named_scope("image_x"):
        r1, r3, r2 = (send(m, along_x(k)) for m, k in ((m1, 1), (m3, 3), (m2, 2)))
    with jax.named_scope("panel_across"):
        across = send(after(across, grams), planes(0), lambda x, core, z, y: core == y // 2)
    with jax.named_scope("factor"):
        gram, upper, upper_here = local(factor_kernel, [tile] * 3, 4, [pltpu.VMEM((WIDTH, WIDTH), F32)], 2000000000)(
            *grams
        )
    r1, r3, r2 = after((r1, r3, r2), upper_here)
    with jax.named_scope("image_x"):
        image, normal = local(combine_kernel, [shape(PIECE), tile], 4)(m0, r1, r3, r2, gram, upper_here)

    with jax.named_scope("image_planes"):
        planes_in = [send(image, planes(k)) for k in (0, 1, 3, 2)]
    with jax.named_scope("panel_across"):
        handed = send(local(hand_kernel, shape(PIECE), 4)(place, after(across, planes_in[3])), other_core)
    with jax.named_scope("image_planes"):
        in_plane = local(join_z_kernel, shape(4 * PIECE), 4)(place, *after(planes_in, handed))
    with jax.named_scope("image_y"):
        below, above = send(in_plane, turn(along_y, 1)), send(in_plane, turn(along_y, 3))
    with jax.named_scope("image_columns"):
        tagged = local(tag_kernel, shape(2 * PIECE), 4)(place, image, across, handed)
        sides = ring(tagged, along_x)
    with jax.named_scope("inverse"):
        inverse = local(inverse_kernel, tile, 4, flops=2000000000)(after(normal, in_plane))
    below = after(below, inverse, sides[0])
    with jax.named_scope("image_far"):
        opposite = send(below, turn(along_y, 1))
    blocks = [in_plane, below, above, opposite]
    with jax.named_scope("pick"):
        chosen = local(pick_kernel, shape(8 * PIECE), 8)(place, *blocks)
    with jax.named_scope("image_swap"):
        swapped = send(chosen, other_core)
    with jax.named_scope("image_columns"):
        own = local(untag_kernel, shape(8 * PIECE), 8)(place, tagged, *after(sides, chosen))
        other = send(own, other_core)
    with jax.named_scope("gather"):
        shifted, image_rows, inner = local(gather_kernel, [shape(ROWS), shape(ROWS), tile], 16)(
            place, *in_z, upper_here, *blocks, swapped
        )
    with jax.named_scope("inner"):
        inner = inner + send(inner, other_core)
        k1, k3, k2 = ring(inner, along_x)

    with jax.named_scope("first_update"):
        base, turned = local(
            first_update_kernel,
            [shape(ROWS, COLS), shape(WIDTH, COLS)],
            24,
            [
                pltpu.VMEM((COLS, WIDTH), F32),
                pltpu.VMEM((COLS, WIDTH), F32),
                pltpu.VMEM((2 * WIDTH, COLS), BF16),
                pltpu.VMEM((2 * WIDTH, COLS), BF16),
                pltpu.VMEM((ROWS, WIDTH), F32),
            ],
            12 * ROWS * COLS * WIDTH,
        )(place, whole, shifted, image_rows, own, other, upper_here, after(inverse, inner))
    k1, k3, k2 = after((k1, k3, k2), base)
    with jax.named_scope("last_update"):
        updated = pl.pallas_call(
            last_update_kernel,
            in_specs=[VMEM] * 8,
            out_specs=anywhere,
            out_shape=shape(ROWS, COLS),
            scratch_shapes=[
                pltpu.VMEM((2 * WIDTH, COLS), BF16),
                pltpu.VMEM((WIDTH, COLS), BF16),
                pltpu.VMEM((ROWS, COLS), F32),
                pltpu.SemaphoreType.DMA((ROWS // WIDTH,)),
            ],
            compiler_params=params(20),
            cost_estimate=pl.CostEstimate(flops=8 * ROWS * COLS * WIDTH, bytes_accessed=4 * ROWS * COLS, transcendentals=0),
        )(base, shifted, turned, inverse, inner, k1, k3, k2)
    return upper, updated


def solution(mesh):
    return jax.shard_map(
        shards,
        mesh=mesh,
        in_specs=(P(("row", "col"), None), P("row", "col")),
        out_specs=(P(), P("row", "col")),
        check_vma=False,
    )
```

```python
import jax
import jax.numpy as jnp
from jax import lax
from jax.experimental import pallas as pl
from jax.experimental.pallas import tpu as pltpu
from jax.sharding import PartitionSpec as P

F32 = jnp.float32
BF16 = jnp.bfloat16
AXES = ("row", "col")
PIECE = 144
WIDTH = 128
ROWS = 16 * PIECE
COLS = 8 * PIECE
TALL = 256
STEPS = ROWS // TALL
VMEM = pl.BlockSpec(memory_space=pltpu.VMEM)
SMEM = pl.BlockSpec(memory_space=pltpu.SMEM)


def pairs(where, only=None):
    result = []
    for x in range(4):
        for core in range(2):
            for z in range(4):
                for y in range(4):
                    if only is not None and not only(x, core, z, y):
                        continue
                    tx, tcore, tz, ty = where(x, core, z, y)
                    source = (2 * x + core) * 16 + 4 * z + y
                    target = (2 * tx + tcore) * 16 + 4 * tz + ty
                    result.append((source, target))
    return result


def send(value, where, only=None):
    return lax.ppermute(value, AXES, pairs(where, only))


def along_x(k):
    return lambda x, core, z, y: ((x + k) % 4, core, z, y)


def along_z(k):
    return lambda x, core, z, y: (x, core, (z + k) % 4, y)


def along_y(k):
    return lambda x, core, z, y: (x, core, z, (y + k) % 4)


def other_core(x, core, z, y):
    return (x, 1 - core, z, y)


def planes(k):
    return lambda x, core, z, y: (z, core, (x + k) % 4, y)


def read_across(x, core, z, y):
    return core == y // 2


def ring(value, direction):
    return [send(value, direction(k)) for k in (1, 3, 2)]


def halves(value):
    high = value.astype(BF16)
    return high, (value - high.astype(F32)).astype(BF16)


def dot16(left, right, dims):
    return lax.dot_general(left, right, (dims, ((), ())), preferred_element_type=F32)


def split_dot(left, right, dims):
    left_high, left_low = halves(left)
    right_high, right_low = halves(right)
    return (
        dot16(left_low, right_high, dims)
        + dot16(left_high, right_low, dims)
        + dot16(left_high, right_high, dims)
    )


def full_dot(left, right, dims=((1,), (0,))):
    return lax.dot_general(
        left, right, (dims, ((), ())), precision=lax.Precision.HIGHEST, preferred_element_type=F32
    )


def lane(value, index):
    return jnp.take_along_axis(value, jnp.full(value.shape, index, jnp.int32), axis=1)


ALONG = (0, 1, 3, 2)


def around(core):
    return (0, 1 + 2 * core, 3 - 2 * core, 2)


def put_in_order(at, steps, pieces, out, rows, first=0):
    for k, piece in zip(steps, pieces):
        start = pl.multiple_of(first + ((at - k + 4) % 4) * rows, 16)
        out[pl.ds(start, rows), :] = piece[...]


def join_y_kernel(place, p0, p1, p3, p2, out):
    put_in_order(place[3], ALONG, (p0, p1, p3, p2), out, PIECE)


def join_z_kernel(place, p0, p1, p3, p2, out):
    put_in_order(place[2], ALONG, (p0, p1, p3, p2), out, PIECE)


def hand_kernel(place, across, out):
    out[...] = across[pl.ds(pl.multiple_of((1 - place[1]) * PIECE, 16), PIECE), :]


def tag_kernel(place, image, across, handed, out):
    out[:PIECE, :] = image[...]

    @pl.when(place[3] // 2 == place[1])
    def _():
        out[PIECE:, :] = across[pl.ds(pl.multiple_of(place[1] * PIECE, 16), PIECE), :]

    @pl.when(place[3] // 2 != place[1])
    def _():
        out[PIECE:, :] = handed[...]


def split_kernel(trailing, after, whole, high, low, sems):
    copies = []
    for i in range(STEPS):
        rows = pl.ds(i * TALL, TALL)
        copies.append(pltpu.make_async_copy(trailing.at[rows, :], whole.at[rows, :], sems.at[i]))
        copies[-1].start()
    for i in range(STEPS):
        copies[i].wait()
        rows = slice(i * TALL, (i + 1) * TALL)
        high[rows, :], low[rows, :] = halves(whole[rows, :])


def turned_image(place, k, block, high, low):
    rows = pl.ds(pl.multiple_of(((place[2] - k + 4) % 4) * 4 * PIECE, 16), 4 * PIECE)
    turned_high, turned_low = halves(block[...].T)
    wide = dot16(jnp.concatenate([turned_high, turned_low], axis=0), high[rows, :], ((1,), (0,)))
    return wide[:WIDTH] + wide[WIDTH:] + dot16(turned_high, low[rows, :], ((1,), (0,)))


def near_kernel(place, high, low, own, front, back, image, gram, gram_near):
    total = jnp.zeros((WIDTH, COLS), F32)
    for k, block in zip(around(place[1]), (own, front, back)):
        total += turned_image(place, k, block, high, low)
    image[...] = total
    gram[...] = full_dot(own[...], own[...], ((0,), (0,)))
    gram_near[...] = full_dot(front[...], front[...], ((0,), (0,))) + full_dot(back[...], back[...], ((0,), (0,)))


def image_kernel(place, whole, high, low, near, gram, gram_near, own, front, back, far, sent, kept, across):
    blocks = (own, front, back, far)
    total = (gram[...] + full_dot(far[...], far[...], ((0,), (0,)))) + gram_near[...]
    for out in (sent, kept):
        out[8 * PIECE : 8 * PIECE + WIDTH, :] = total
        out[8 * PIECE + WIDTH :, :] = jnp.zeros((WIDTH, WIDTH), F32)
    for k, piece in zip(around(place[1]), blocks):

        @pl.when((place[0] == 0) & (place[1] == 0) & (place[2] == k))
        def _(piece=piece):
            kept[8 * PIECE + WIDTH :, :] = piece[:WIDTH, :]
            sent[8 * PIECE + WIDTH :, :] = piece[:WIDTH, :]

    image = (near[...] + turned_image(place, 2, far, high, low)).T
    block, half = 2 * (place[3] % 2) + place[2] // 2, place[2] % 2
    for k, piece in zip(around(place[1]), blocks):

        @pl.when((place[2] - k + 4) % 4 == block)
        def _(piece=piece):
            across[...] = piece[pl.ds(pl.multiple_of(half * 2 * PIECE, 16), 2 * PIECE), :]

    corner = whole[:WIDTH, :].T * jnp.where((place[0] == 0) & (place[1] == 0), 1.0, 0.0)
    for out, half in ((kept, place[1]), (sent, 1 - place[1])):
        for value in range(2):

            @pl.when(half == value)
            def _(out=out, value=value):
                for x in range(4):
                    index = (2 * x + value) * PIECE
                    out[x * PIECE : (x + 1) * PIECE, :] = image[index : index + PIECE, :]
                    out[(4 + x) * PIECE : (5 + x) * PIECE, :] = corner[index : index + PIECE, :]


def factor_kernel(own, r1, r3, r2, gram, upper, upper_here, work):
    total = (own[...] + r2[...]) + (r1[...] + r3[...])
    gram[...] = total
    work[...] = total
    cholesky_rows(work, upper_here)
    upper[...] = upper_here[...]


def combine_kernel(own, r1, r3, r2, gram, upper, image, normal):
    total = (own[...] + r2[...]) + (r1[...] + r3[...])
    image[...] = total[:PIECE, :] + split_dot(total[PIECE : 2 * PIECE, :], upper[...], ((1,), (0,)))
    normal[...] = gram[...] + full_dot(total[2 * PIECE :, :], upper[...], ((0,), (0,)))


def deal_kernel(place, kept, received, small, m0, m1, m3, m2):
    small[...] = kept[8 * PIECE : 8 * PIECE + WIDTH, :] + received[8 * PIECE : 8 * PIECE + WIDTH, :]
    top = kept[8 * PIECE + WIDTH :, :] + received[8 * PIECE + WIDTH :, :]
    for k, out in ((0, m0), (1, m1), (3, m3), (2, m2)):
        for part in range(2):
            start = pl.multiple_of((4 * part + (place[0] + k) % 4) * PIECE, 16)
            rows = pl.ds(start, PIECE)
            out[part * PIECE : (part + 1) * PIECE, :] = kept[rows, :] + received[rows, :]
        out[2 * PIECE :, :] = top


def untag_kernel(place, p0, p1, p3, p2, out):
    pieces = (p0, p1, p3, p2)
    put_in_order(place[0], ALONG, [p.at[:PIECE, :] for p in pieces], out, PIECE)
    put_in_order(place[0], ALONG, [p.at[PIECE:, :] for p in pieces], out, PIECE, 4 * PIECE)


def cholesky_rows(work, factor):
    lanes = lax.broadcasted_iota(jnp.int32, (1, WIDTH), 1)
    subs = lax.broadcasted_iota(jnp.int32, (8, 1), 0)

    def body(t, carry):
        first = pl.multiple_of(8 * t, 8)
        whole = work[...]
        block = work[pl.ds(first, 8), :]
        columns = [lane(whole, first + b) for b in range(8)]
        pivots = [lane(block, first + b) for b in range(8)]
        for i in range(8):
            row, pivot = block[i : i + 1], pivots[i][i : i + 1]
            inverse = 1.0 / pivot
            scaled = row * lax.rsqrt(pivot)
            factor[pl.ds(first + i, 1), :] = jnp.where(lanes >= first + i, scaled, 0.0)
            column, here = pivots[i], subs == i
            row = row * inverse
            block = jnp.where(here, row, block - column * row)
            for b in range(i + 1, 8):
                entry = pivots[b][i : i + 1] * inverse
                pivots[b] = jnp.where(here, entry, pivots[b] - column * entry)
        for i in range(8):
            whole = whole - columns[i] * block[i : i + 1]
        work[...] = whole
        return carry

    lax.fori_loop(0, WIDTH // 8, body, 0)


def inverse_kernel(source, out):
    out[...] = source[...]
    lanes = lax.broadcasted_iota(jnp.int32, (1, WIDTH), 1)
    subs = lax.broadcasted_iota(jnp.int32, (8, 1), 0)

    def body(t, carry):
        first = pl.multiple_of(8 * t, 8)
        whole = out[...]
        block = out[pl.ds(first, 8), :]
        columns = [lane(whole, first + b) for b in range(8)]
        pivots = [lane(block, first + b) for b in range(8)]
        for i in range(8):
            row, column, here = block[i : i + 1], pivots[i], subs == i
            inverse = 1.0 / column[i : i + 1]
            is_lane = lanes == first + i
            row = jnp.where(is_lane, inverse, row * inverse)
            block = jnp.where(here, row, jnp.where(is_lane, 0.0, block) - column * row)
            for b in range(8):
                if b != i:
                    entry = pivots[b][i : i + 1] * inverse
                    pivots[b] = jnp.where(here, entry, pivots[b] - column * entry)
            pivots[i] = jnp.where(here, inverse, -column * inverse)
        whole = jnp.where((lanes >= first) & (lanes < first + 8), 0.0, whole)
        for i in range(8):
            whole = whole - columns[i] * block[i : i + 1]
        out[...] = whole
        out[pl.ds(first, 8), :] = block
        return carry

    lax.fori_loop(0, WIDTH // 8, body, 0)


def pick_kernel(place, b0, b1, b3, b2, out):
    core, y = place[1], place[3]
    for part in range(2):
        wanted = (y - (2 * (1 - core) + part) + 4) % 4
        for k, block in zip(around(core), (b0, b1, b3, b2)):

            @pl.when(wanted == k)
            def _(block=block, part=part):
                out[part * 4 * PIECE : (part + 1) * 4 * PIECE, :] = block[...]


def gather_kernel(place, p0, p1, p3, p2, upper, b0, b1, b3, b2, swapped, shifted, image_rows, inner):
    x, core, z, y = place[0], place[1], place[2], place[3]
    first = jnp.where((x == 0) & (core == 0), 1.0, 0.0)
    put_in_order(z, around(core), (p0, p1, p3, p2), shifted, 4 * PIECE)
    shifted[:WIDTH, :] += upper[...] * first

    def put(block, offset, part, half):
        for other in range(4):
            start = pl.multiple_of((8 * part + 2 * other + half) * PIECE, 16)
            piece = offset + other * PIECE
            image_rows[pl.ds(start, PIECE), :] = block[piece : piece + PIECE, :]

    for part in range(2):
        wanted = (y - (2 * core + part) + 4) % 4
        for k, block in zip(around(core), (b0, b1, b3, b2)):

            @pl.when(wanted == k)
            def _(block=block, part=part):
                put(block, 0, part, core)

        put(swapped, part * 4 * PIECE, part, 1 - core)
    inner[...] = split_dot(shifted[...], image_rows[...], ((0,), (0,)))


def cols_of(place, own, swapped, target, part):
    for half, block in ((place[1], own), (1 - place[1], swapped)):
        for x in range(4):
            start = pl.multiple_of((2 * x + half) * PIECE, 16)
            piece = (4 * part + x) * PIECE
            target[pl.ds(start, PIECE), :] = block[piece : piece + PIECE, :]


def wide_dot(left, right):
    left_high, left_low = halves(left)
    right_high, right_low = halves(right)
    width = right.shape[1]
    both = dot16(left_high, jnp.concatenate([right_high, right_low], axis=1), ((1,), (0,)))
    return both[:, :width] + both[:, width:] + dot16(left_low, right_high, ((1,), (0,)))


def first_update_kernel(
    place, whole, shifted_rows, image_rows, own, swapped, upper, inverse,
    result, turned, panel_cols, image_cols, right_high, right_low, w_rows,
):
    cols_of(place, own, swapped, image_cols, 0)
    cols_of(place, own, swapped, panel_cols, 1)
    first = jnp.where((place[2] == 0) & (place[3] == 0), 1.0, 0.0)
    panel_cols[:WIDTH, :] += upper[...] * first
    turned[...] = panel_cols[...].T
    w_cols = wide_dot(image_cols[...], inverse[...])
    right_high[:WIDTH, :], right_low[:WIDTH, :] = halves(w_cols.T)
    right_high[WIDTH:, :], right_low[WIDTH:, :] = halves(turned[...])
    w_rows[...] = wide_dot(image_rows[...], inverse[...])
    dims = ((1,), (0,))
    for i in range(ROWS // WIDTH):
        rows = slice(i * WIDTH, (i + 1) * WIDTH)
        left_high, left_low = halves(jnp.concatenate([shifted_rows[rows, :], w_rows[rows, :]], axis=1))
        change = dot16(left_low, right_high[...], dims) + dot16(left_high, right_low[...], dims)
        result[rows, :] = whole[rows, :] - (change + dot16(left_high, right_high[...], dims))


def last_update_kernel(base, shifted_rows, turned, inverse, k0, k1, k3, k2, out, right, right_low, result, sems):
    inner = (k0[...] + k2[...]) + (k1[...] + k3[...])
    dims = ((1,), (0,))
    core_block = split_dot(split_dot(inverse[...], inner, ((0,), (0,))), inverse[...], dims)
    high, low = halves(split_dot(core_block, turned[...], dims))
    right[:WIDTH, :] = high
    right[WIDTH:, :] = high
    right_low[...] = low
    copies = []
    for i in range(ROWS // WIDTH):
        rows = slice(i * WIDTH, (i + 1) * WIDTH)
        left_high, left_low = halves(shifted_rows[rows, :])
        change = dot16(jnp.concatenate([left_high, left_low], axis=1), right[...], dims)
        result[rows, :] = base[rows, :] + (change + dot16(left_high, right_low[...], dims))
        rows = pl.ds(i * WIDTH, WIDTH)
        copies.append(pltpu.make_async_copy(result.at[rows, :], out.at[rows, :], sems.at[i]))
        copies[-1].start()
    for copy in copies:
        copy.wait()


def shape(rows, columns=WIDTH):
    return jax.ShapeDtypeStruct((rows, columns), F32)


def params(mib):
    return pltpu.CompilerParams(vmem_limit_bytes=mib * 1024 * 1024)


def local(kernel, out_shape, mib, scratch=(), flops=0):
    cost = pl.CostEstimate(flops=flops, bytes_accessed=0, transcendentals=0) if flops else None

    def run(*operands):
        specs = [SMEM if value.dtype == jnp.int32 else VMEM for value in operands]
        outs = [VMEM] * len(out_shape) if isinstance(out_shape, list) else VMEM
        return pl.pallas_call(
            kernel, in_specs=specs, out_specs=outs, out_shape=out_shape, scratch_shapes=list(scratch),
            compiler_params=params(mib), cost_estimate=cost,
        )(*operands)

    return run


def turn(axis, first):
    def where(x, core, z, y):
        return axis(first if core == 0 else 4 - first)(x, core, z, y)

    return where


def after(values, *earlier):
    return lax.optimization_barrier((values, earlier))[0]


def shards(panel, trailing):
    row, col = lax.axis_index("row"), lax.axis_index("col")
    place = jnp.stack([row // 2, row % 2, col // 4, col % 4]).astype(jnp.int32)
    anywhere = pl.BlockSpec(memory_space=pl.ANY)
    tile = shape(WIDTH)
    tile16 = jax.ShapeDtypeStruct((ROWS, COLS), BF16)

    with jax.named_scope("panel_y"):
        in_y = local(join_y_kernel, shape(4 * PIECE), 4)(place, panel, *ring(panel, along_y))
    with jax.named_scope("panel_z"):
        below, above = send(in_y, turn(along_z, 1)), send(in_y, turn(along_z, 3))
    with jax.named_scope("split"):
        whole, high, low = pl.pallas_call(
            split_kernel,
            in_specs=[anywhere, VMEM],
            out_specs=[VMEM] * 3,
            out_shape=[shape(ROWS, COLS), tile16, tile16],
            scratch_shapes=[pltpu.SemaphoreType.DMA((STEPS,))],
            compiler_params=params(24),
            cost_estimate=pl.CostEstimate(flops=0, bytes_accessed=4 * ROWS * COLS, transcendentals=0),
        )(trailing, in_y)
    below, above = after((below, above), whole)
    with jax.named_scope("panel_far"):
        far = send(below, turn(along_z, 1))
    with jax.named_scope("near"):
        near, gram, gram_near = local(near_kernel, [shape(WIDTH, COLS), tile, tile], 16, flops=5 * ROWS * COLS * WIDTH)(
            place, high, low, in_y, below, above
        )
    far = after(far, gram)
    in_z = [in_y, below, above, far]

    with jax.named_scope("image"):
        sent, kept, across = local(
            image_kernel, [shape(8 * PIECE + 2 * WIDTH)] * 2 + [shape(2 * PIECE)], 24, flops=2 * ROWS * COLS * WIDTH
        )(place, whole, high, low, near, gram, gram_near, *in_z)
    with jax.named_scope("image_core"):
        received = send(sent, other_core)
    with jax.named_scope("deal"):
        gram, m0, m1, m3, m2 = local(deal_kernel, [tile] + [shape(2 * PIECE + WIDTH)] * 4, 8)(place, kept, received)
    with jax.named_scope("gram_x"):
        grams = [gram] + ring(gram, along_x)
    with jax.named_scope("image_x"):
        r1, r3, r2 = (send(m, along_x(k)) for m, k in ((m1, 1), (m3, 3), (m2, 2)))
    with jax.named_scope("panel_across"):
        across = send(after(across, grams), planes(0), read_across)
    with jax.named_scope("factor"):
        gram, upper, upper_here = local(factor_kernel, [tile] * 3, 4, [pltpu.VMEM((WIDTH, WIDTH), F32)], 2000000000)(
            *grams
        )
    r1, r3, r2 = after((r1, r3, r2), upper_here)
    with jax.named_scope("image_x"):
        image, normal = local(combine_kernel, [shape(PIECE), tile], 4)(m0, r1, r3, r2, gram, upper_here)

    with jax.named_scope("image_planes"):
        planes_in = [send(image, planes(k)) for k in (0, 1, 3, 2)]
    with jax.named_scope("panel_across"):
        handed = send(local(hand_kernel, shape(PIECE), 4)(place, after(across, planes_in[3])), other_core, read_across)
    with jax.named_scope("image_planes"):
        in_plane = local(join_z_kernel, shape(4 * PIECE), 4)(place, *after(planes_in, handed))
    with jax.named_scope("image_y"):
        below, above = send(in_plane, turn(along_y, 1)), send(in_plane, turn(along_y, 3))
    with jax.named_scope("image_columns"):
        tagged = local(tag_kernel, shape(2 * PIECE), 4)(place, image, across, handed)
        sides = ring(tagged, along_x)
    with jax.named_scope("inverse"):
        inverse = local(inverse_kernel, tile, 4, flops=2000000000)(after(normal, in_plane))
    below = after(below, inverse, sides[0])
    with jax.named_scope("image_far"):
        opposite = send(below, turn(along_y, 1))
    blocks = [in_plane, below, above, opposite]
    with jax.named_scope("pick"):
        chosen = local(pick_kernel, shape(8 * PIECE), 8)(place, *blocks)
    with jax.named_scope("image_swap"):
        swapped = send(chosen, other_core)
    with jax.named_scope("image_columns"):
        own = local(untag_kernel, shape(8 * PIECE), 8)(place, tagged, *after(sides, chosen))
        other = send(own, other_core)
    with jax.named_scope("gather"):
        shifted, image_rows, inner = local(gather_kernel, [shape(ROWS), shape(ROWS), tile], 16)(
            place, *in_z, upper_here, *blocks, swapped
        )
    with jax.named_scope("inner"):
        inner = inner + send(inner, other_core)
        k1, k3, k2 = ring(inner, along_x)

    with jax.named_scope("first_update"):
        base, turned = local(
            first_update_kernel,
            [shape(ROWS, COLS), shape(WIDTH, COLS)],
            24,
            [
                pltpu.VMEM((COLS, WIDTH), F32),
                pltpu.VMEM((COLS, WIDTH), F32),
                pltpu.VMEM((2 * WIDTH, COLS), BF16),
                pltpu.VMEM((2 * WIDTH, COLS), BF16),
                pltpu.VMEM((ROWS, WIDTH), F32),
            ],
            12 * ROWS * COLS * WIDTH,
        )(place, whole, shifted, image_rows, own, other, upper_here, after(inverse, inner))
    k1, k3, k2 = after((k1, k3, k2), base)
    with jax.named_scope("last_update"):
        updated = pl.pallas_call(
            last_update_kernel,
            in_specs=[VMEM] * 8,
            out_specs=anywhere,
            out_shape=shape(ROWS, COLS),
            scratch_shapes=[
                pltpu.VMEM((2 * WIDTH, COLS), BF16),
                pltpu.VMEM((WIDTH, COLS), BF16),
                pltpu.VMEM((ROWS, COLS), F32),
                pltpu.SemaphoreType.DMA((ROWS // WIDTH,)),
            ],
            compiler_params=params(20),
            cost_estimate=pl.CostEstimate(flops=8 * ROWS * COLS * WIDTH, bytes_accessed=4 * ROWS * COLS, transcendentals=0),
        )(base, shifted, turned, inverse, inner, k1, k3, k2)
    return upper, updated


def solution(mesh):
    return jax.shard_map(
        shards,
        mesh=mesh,
        in_specs=(P(("row", "col"), None), P("row", "col")),
        out_specs=(P(), P("row", "col")),
        check_vma=False,
    )
```
